32 devices in a mesh: rep: 2 (over x), node: 4 (over y, core), local: 4 (over z).
Axes of the slice: x: 2, y: 2, z: 4, core: 2. Of those that a mesh axis runs over, the one named last changes fastest.
Arguments:
- grad_out: bfloat16 [512, 3584], P(('rep', 'node', 'local')), parts along dimension 0, may hold values from -6 to 6
- saved_input: bfloat16 [512, 3584], P(('rep', 'node', 'local')), parts along dimension 0, may hold values from -6 to 6
- gate_weight: bfloat16 [8, 3584, 1024], P('node', None, 'local'), may hold values from -0.09375 to 0.09375
- up_weight: bfloat16 [8, 3584, 1024], P('node', None, 'local'), may hold values from -0.09375 to 0.09375
- down_weight: bfloat16 [8, 1024, 3584], P('node', 'local'), may hold values from -0.1875 to 0.1875
- expert_ids: int32 [512, 6], P(('rep', 'node', 'local')), parts along dimension 0, may hold values from 0 to 7, as said below
- gate_num: int32 [512, 6], P(('rep', 'node', 'local')), parts along dimension 0, may hold values from 16 to 255
Outputs:
- grad_input: bfloat16 [512, 3584], P(('rep', 'node', 'local')), parts along dimension 0
- grad_gate_weight: bfloat16 [16, 3584, 1024], P(('rep', 'node'), None, 'local'), parts along dimension 0
- grad_up_weight: bfloat16 [16, 3584, 1024], P(('rep', 'node'), None, 'local'), parts along dimension 0
- grad_down_weight: bfloat16 [16, 1024, 3584], P(('rep', 'node'), 'local'), parts along dimension 0
The draws below stay inside these ranges and needn't reach their ends.
There are 2 independent parts, one for each index of `rep`. The reference program is written for one: setup_inputs(seed, part) draws one part's arguments, and reference() takes and returns one part's arrays. A program takes and returns all parts, laid end to end along the dimension named above; an argument that names none is the same for every part. Nothing has to cross between parts.
Inputs may be any that keep to these rules, and one draw needn't show every extreme that they name: `expert_ids`: each token names 6 different experts lying in exactly 4 node groups (expert e in group e // 2): both experts of 2 of these groups and one expert of each other. Of the 16 tokens of one device, at most 16 visit any one node group; one node group is visited by exactly 16 tokens of every device.
All inputs are finite; a program needn't handle non-finite values.
Results may differ from the reference program's by a relative error of at most 0.0064.
Values may be sent and summed in bfloat16 or wider, within the bound.
No kernel may reach another device: no remote copies, remote signals or barrier semaphores. Data moves between devices by JAX's collectives and lax.ppermute only.
A program may use at most 192 MiB of HBM per device.

```python
import jax
import jax.numpy as jnp
from jax import lax

D = 3584
F = 1024
EPG = 2
TOPK = 6
LIMIT = 4
TOK_DEV = 16
TOKENS = 256
EXPERTS = 8
CAP = 16
SLOTS = 256
N_NODE = 4


def draw_expert_ids(key, part):
    key = jax.random.fold_in(key, 7)
    key_list = jax.random.split(key, 5)
    devices = TOKENS // TOK_DEV
    groups = EXPERTS // EPG
    popular = jax.random.permutation(key_list[0], groups).astype(jnp.int32)
    jitter = jax.random.randint(key_list[1], (devices, groups), 1, 9).astype(jnp.int32)
    jitter = jnp.where(popular[None, :] == 0, 0, jitter)
    rank_score = (popular[None, :] * 4 + jitter) * groups + jnp.arange(groups, dtype=jnp.int32)[None, :]
    by_rank = jnp.argsort(rank_score, axis=1).astype(jnp.int32)
    least_len = max(0, min(CAP, -(-(LIMIT * TOK_DEV - CAP) // (groups - 1))))
    other_len = jax.random.randint(key_list[2], (devices, groups - 1), least_len, CAP + 1).astype(jnp.int32)
    lengths = jnp.concatenate([jnp.full((devices, 1), CAP, jnp.int32), other_len], axis=1)
    run_ends = jnp.cumsum(lengths, axis=1)
    places = jnp.arange(LIMIT * TOK_DEV, dtype=jnp.int32)
    run_index = jnp.sum((run_ends[:, None, :] <= places[None, :, None]).astype(jnp.int32), axis=2)
    chosen = jnp.take_along_axis(by_rank, run_index, axis=1)
    visited = jnp.transpose(chosen.reshape(devices, LIMIT, TOK_DEV), (0, 2, 1))
    mixing = jax.random.randint(key_list[3], (devices, TOK_DEV, LIMIT), 0, 1 << 20).astype(jnp.int32) * LIMIT
    mixing = mixing + jnp.arange(LIMIT, dtype=jnp.int32)[None, None, :]
    visited = jnp.take_along_axis(visited, jnp.argsort(mixing, axis=2).astype(jnp.int32), axis=2)
    doubles = TOPK - LIMIT
    single_pick = jax.random.randint(key_list[4], (devices, TOK_DEV, LIMIT), 0, EPG).astype(jnp.int32)
    both_ids = jnp.stack([visited[..., :doubles] * EPG, visited[..., :doubles] * EPG + 1], axis=-1)
    both_ids = both_ids.reshape(devices, TOK_DEV, 2 * doubles)
    single_ids = visited[..., doubles:] * EPG + single_pick[..., doubles:]
    return jnp.concatenate([both_ids, single_ids], axis=-1).reshape(TOKENS, TOPK).astype(jnp.int32)


def set_ends(array, stream_key, low, largest):
    spot = [jax.random.randint(jax.random.fold_in(stream_key, axis), (), 0, length) for axis, length in enumerate(array.shape)]
    main_axis = array.shape.index(max(array.shape))
    beside = spot[:main_axis] + [(spot[main_axis] + 1) % array.shape[main_axis]] + spot[main_axis + 1:]
    return array.at[tuple(spot)].set(low).at[tuple(beside)].set(largest)


def block_levels(stream_key, shape, cuts, least, high):
    factor_of = 1.0
    for axis_at, shards_of in cuts:
        steps = jax.random.uniform(jax.random.fold_in(jax.random.fold_in(stream_key, 6), axis_at), (shards_of,), jnp.float32, least / len(cuts), high / len(cuts))
        factor_of = factor_of * jnp.repeat(jnp.exp(steps), shape[axis_at] // shards_of).reshape((-1,) + (1,) * (len(shape) - 1 - axis_at))
    return factor_of


def gaussian(key, extent, deviation, bound, pieces=(), kind=jnp.bfloat16):
    values = deviation * jax.random.normal(key, extent, jnp.float32)
    if pieces:
        values = values * block_levels(key, extent, pieces, -0.22, 0.18)
    return jnp.clip(values, -bound, bound).astype(kind)


def setup_inputs(seed: int = 0, part: int = 0) -> dict:
    keys = jax.random.split(jax.random.key(seed), 8)
    part_keys = jax.random.split(jax.random.fold_in(keys[7], part), 8)
    return {
        "grad_out": gaussian(part_keys[0], (TOKENS, D), 1.0, 6.0, ((0, 16),)),
        "saved_input": gaussian(part_keys[1], (TOKENS, D), 1.0, 6.0, ((0, 16),)),
        "gate_weight": gaussian(keys[2], (EXPERTS, D, F), D ** -0.5, 0.09375, ((0, 4), (2, 4))),
        "up_weight": gaussian(keys[3], (EXPERTS, D, F), D ** -0.5, 0.09375, ((0, 4), (2, 4))),
        "down_weight": gaussian(keys[4], (EXPERTS, F, D), F ** -0.5, 0.1875, ((0, 4), (1, 4))),
        "expert_ids": draw_expert_ids(jax.random.fold_in(jax.random.fold_in(keys[7], part), 71), part),
        "gate_num": set_ends(jax.random.randint(part_keys[6], (TOKENS, TOPK), 16, 256), jax.random.fold_in(part_keys[6], 1), 16, 255).astype(jnp.int32),
    }


gate_scale = 1.0 / 256.0


def reference(grad_out, saved_input, gate_weight, up_weight, down_weight, expert_ids, gate_num):
    expert_hot = (expert_ids[:, :, None] == jnp.arange(EXPERTS, dtype=jnp.int32)[None, None, :]).astype(jnp.float32)
    gate_values = jnp.sum(expert_hot * (gate_num.astype(jnp.float32) * gate_scale)[:, :, None], axis=1)
    group_of = expert_ids // EPG

    def per_group(group):
        visits = jnp.any(group_of == group, axis=1).astype(jnp.int32)
        by_slot = jnp.argsort(1 - visits, stable=True)[:SLOTS].astype(jnp.int32)
        filled = visits[by_slot]
        inputs = saved_input[by_slot] * filled[:, None].astype(saved_input.dtype)
        row_grads = grad_out[by_slot] * filled[:, None].astype(grad_out.dtype)
        own_gates = lax.dynamic_slice_in_dim(gate_values, (group * EPG).astype(jnp.int32), EPG, 1)
        row_gates = own_gates[by_slot] * filled[:, None].astype(jnp.float32)
        start = (group * EPG).astype(jnp.int32)
        gate_here = lax.dynamic_slice_in_dim(gate_weight, start, EPG, 0)
        up_here = lax.dynamic_slice_in_dim(up_weight, start, EPG, 0)
        down_here = lax.dynamic_slice_in_dim(down_weight, start, EPG, 0)
        summed = jnp.zeros((SLOTS, D), jnp.float32)
        gate_grads = []
        up_grads = []
        down_grads = []
        for expert in range(EPG):
            gate_act = jnp.dot(inputs, gate_here[expert], preferred_element_type=jnp.float32)
            up_act = jnp.dot(inputs, up_here[expert], preferred_element_type=jnp.float32)
            sigmoid_val = jax.nn.sigmoid(gate_act)
            hidden = (gate_act * sigmoid_val * up_act).astype(grad_out.dtype)
            scaled = (row_gates[:, expert:expert + 1] * row_grads.astype(jnp.float32)).astype(grad_out.dtype)
            down_grads.append(jnp.dot(hidden.T, scaled, preferred_element_type=jnp.float32).astype(grad_out.dtype))
            back_grad = jnp.dot(scaled, down_here[expert].T, preferred_element_type=jnp.float32)
            grad_gate_act = (back_grad * up_act * sigmoid_val * (1.0 + gate_act * (1.0 - sigmoid_val))).astype(grad_out.dtype)
            grad_up_act = (back_grad * gate_act * sigmoid_val).astype(grad_out.dtype)
            gate_grads.append(jnp.dot(inputs.T, grad_gate_act, preferred_element_type=jnp.float32).astype(grad_out.dtype))
            up_grads.append(jnp.dot(inputs.T, grad_up_act, preferred_element_type=jnp.float32).astype(grad_out.dtype))
            summed = summed + jnp.dot(grad_gate_act, gate_here[expert].T, preferred_element_type=jnp.float32)
            summed = summed + jnp.dot(grad_up_act, up_here[expert].T, preferred_element_type=jnp.float32)
        group_grad = summed.astype(grad_out.dtype)
        return group_grad, by_slot, filled, jnp.stack(gate_grads), jnp.stack(up_grads), jnp.stack(down_grads)

    group_grads, slots_all, filled_all, gate_all, up_all, down_all = lax.map(per_group, jnp.arange(N_NODE, dtype=jnp.int32))
    values = group_grads.astype(jnp.float32) * filled_all[:, :, None].astype(jnp.float32)
    total = jnp.zeros((TOKENS, D), jnp.float32).at[slots_all.reshape(-1)].add(values.reshape(-1, D))
    grad_input = total.astype(grad_out.dtype)
    return (grad_input, gate_all.reshape(EXPERTS, D, F), up_all.reshape(EXPERTS, D, F), down_all.reshape(EXPERTS, F, D))
```

```python
import jax
import jax.numpy as jnp
from jax import lax
from jax.sharding import PartitionSpec as P

LIMIT = 4


gate_scale = 1.0 / 256.0


def spread_rows(source, groups, local_count):
    widened = jnp.broadcast_to(source[:, None], (groups, local_count) + source.shape[1:])
    return widened.reshape((groups * local_count,) + source.shape[1:])


def slots_per_device(grad_out, saved_input, gate_weight, up_weight, down_weight, expert_ids, gate_num):
    tokens_here = grad_out.shape[0]
    model_width = grad_out.shape[1]
    groups = lax.axis_size("node")
    local_count = lax.axis_size("local")
    experts_here = gate_weight.shape[0]
    capacity = min(tokens_here, 2 * LIMIT * tokens_here // groups)
    group_of = expert_ids // experts_here
    visits = jnp.any(
        group_of[:, :, None] == jnp.arange(groups, dtype=jnp.int32)[None, None, :], axis=1
    ).astype(jnp.int32)
    before = jnp.cumsum(visits, axis=0) - visits
    slot_hit = (before[:, :, None] == jnp.arange(capacity, dtype=jnp.int32)[None, None, :]) & (
        visits[:, :, None] == 1
    )
    select = jnp.transpose(slot_hit, (1, 2, 0)).astype(jnp.bfloat16)
    expert_hot = (
        expert_ids[:, :, None] == jnp.arange(groups * experts_here, dtype=jnp.int32)[None, None, :]
    ).astype(jnp.float32)
    gate_values = jnp.sum(
        expert_hot * (gate_num.astype(jnp.float32) * gate_scale)[:, :, None], axis=1
    )
    gate_table = gate_values.reshape(tokens_here, groups, experts_here)
    send_input = jnp.einsum(
        "gct,td->gcd", select, saved_input, preferred_element_type=jnp.float32
    ).astype(jnp.bfloat16)
    send_grad = jnp.einsum(
        "gct,td->gcd", select, grad_out, preferred_element_type=jnp.float32
    ).astype(jnp.bfloat16)
    send_gate = jnp.einsum("gct,tge->gce", select.astype(jnp.float32), gate_table).astype(
        jnp.bfloat16
    )
    got_input, got_grad, got_gate = (
        lax.all_to_all(
            spread_rows(send_input, groups, local_count),
            ("node", "local"),
            split_axis=0,
            concat_axis=0,
            tiled=True,
        ),
        lax.all_to_all(
            spread_rows(send_grad, groups, local_count),
            ("node", "local"),
            split_axis=0,
            concat_axis=0,
            tiled=True,
        ),
        lax.all_to_all(
            spread_rows(send_gate, groups, local_count),
            ("node", "local"),
            split_axis=0,
            concat_axis=0,
            tiled=True,
        ),
    )
    rows_input = got_input.reshape(groups, local_count, capacity, model_width)
    rows_grad = got_grad.reshape(groups, local_count, capacity, model_width)
    rows_gate = got_gate.reshape(groups, local_count, capacity, experts_here)
    row_count = groups * local_count * capacity
    inputs = rows_input.reshape(row_count, model_width)
    row_grads = rows_grad.reshape(row_count, model_width)
    row_gates = rows_gate.reshape(row_count, experts_here)
    contract_rows = (((0,), (0,)), ((), ()))
    contract_cols = (((1,), (1,)), ((), ()))
    gate_grads = []
    up_grads = []
    down_grads = []
    pieces = []
    columns = []
    for expert in range(experts_here):
        gate_act = jnp.dot(inputs, gate_weight[expert], preferred_element_type=jnp.float32)
        up_act = jnp.dot(inputs, up_weight[expert], preferred_element_type=jnp.float32)
        sigmoid_val = jax.nn.sigmoid(gate_act)
        hidden = (gate_act * sigmoid_val * up_act).astype(jnp.bfloat16)
        scaled = (
            row_gates[:, expert : expert + 1].astype(jnp.float32) * row_grads.astype(jnp.float32)
        ).astype(jnp.bfloat16)
        down_grads.append(
            lax.dot_general(
                hidden, scaled, contract_rows, preferred_element_type=jnp.float32
            ).astype(jnp.bfloat16)
        )
        back_grad = lax.dot_general(
            scaled, down_weight[expert], contract_cols, preferred_element_type=jnp.float32
        )
        grad_gate_act = (
            back_grad * up_act * sigmoid_val * (1.0 + gate_act * (1.0 - sigmoid_val))
        ).astype(jnp.bfloat16)
        grad_up_act = (back_grad * gate_act * sigmoid_val).astype(jnp.bfloat16)
        gate_grads.append(
            lax.dot_general(
                inputs, grad_gate_act, contract_rows, preferred_element_type=jnp.float32
            ).astype(jnp.bfloat16)
        )
        up_grads.append(
            lax.dot_general(
                inputs, grad_up_act, contract_rows, preferred_element_type=jnp.float32
            ).astype(jnp.bfloat16)
        )
        pieces.append(grad_gate_act)
        pieces.append(grad_up_act)
        columns.append(gate_weight[expert])
        columns.append(up_weight[expert])
    activations = jnp.concatenate(pieces, axis=1)
    stacked = jnp.concatenate(columns, axis=1)
    partial_value = lax.dot_general(
        activations, stacked, contract_cols, preferred_element_type=jnp.float32
    )
    returned = lax.all_to_all(
        partial_value.reshape(groups * local_count, capacity, model_width),
        ("node", "local"),
        split_axis=0,
        concat_axis=0,
        tiled=True,
    )
    group_grads = jnp.sum(
        returned.reshape(groups, local_count, capacity, model_width), axis=1
    ).astype(jnp.bfloat16)
    grad_input = jnp.einsum(
        "gct,gcd->td", select, group_grads, preferred_element_type=jnp.float32
    ).astype(jnp.bfloat16)
    return (grad_input, jnp.stack(gate_grads), jnp.stack(up_grads), jnp.stack(down_grads))


def ring_moves(local_count):
    ring_len = 2 * local_count

    def place(core, spot):
        spot = spot % ring_len
        if spot < local_count:
            return core * local_count + spot
        return (2 + core) * local_count + ring_len - 1 - spot

    spots = range(ring_len)
    forth = [(place(0, i), place(0, i + 1)) for i in spots]
    forth += [(place(1, i), place(1, i - 1)) for i in spots]
    back = [(there, here) for here, there in forth]
    swap = [(place(core, i), place(1 - core, i)) for i in spots for core in (0, 1)]
    return forth, back, swap


def move(value, pairs):
    return lax.ppermute(value, ("node", "local"), pairs)


def gather_ring(mine, local_count, moves):
    forth, _, swap = moves
    rows = mine.shape[0]
    other = move(mine, swap)
    block = jnp.concatenate([mine, other], axis=0)
    near = [mine]
    far = [other]
    for _ in range(local_count - 1):
        block = move(block, forth)
        near.append(block)
        far.append(move(block, swap))
    last = move(block[:rows], forth)
    near.append(last)
    far.append(move(last, swap))
    return jnp.concatenate(near + far, axis=0)


def reduce_ring(partial_value, local_count, moves):
    _, back, swap = moves
    total_rows = partial_value.shape[0]
    half = total_rows // 2
    rows = half // (2 * local_count)
    wide = jnp.float32
    from_other = move(partial_value[half:], swap)

    def own(start, count):
        return partial_value[start : start + count].astype(wide) + from_other[
            start : start + count
        ].astype(wide)

    start = half - rows
    moving = move(own(start, rows).astype(jnp.bfloat16), back)
    for _ in range(local_count - 1):
        start -= 2 * rows
        held = own(start, 2 * rows)
        arrived = moving.astype(wide)
        if arrived.shape[0] == rows:
            held = jnp.concatenate([held[:rows] + arrived, held[rows:]], axis=0)
        else:
            held = held + arrived
        moving = move(held.astype(jnp.bfloat16), back)
    crossed = move(moving[rows:], swap)
    return (own(0, rows) + moving[:rows].astype(wide) + crossed.astype(wide)).astype(jnp.bfloat16)


def ring_per_device(
    grad_out, saved_input, gate_weight, up_weight, down_weight, expert_ids, gate_num
):
    model_width = grad_out.shape[1]
    groups = lax.axis_size("node")
    local_count = lax.axis_size("local")
    experts_here = gate_weight.shape[0]
    experts = groups * experts_here
    moves = ring_moves(local_count)
    expert_hot = expert_ids[:, :, None] == jnp.arange(128, dtype=jnp.int32)[None, None, :]
    gates = jnp.sum(
        jnp.where(expert_hot, (gate_num.astype(jnp.float32) * gate_scale)[:, :, None], 0.0), axis=1
    ).astype(jnp.bfloat16)
    grads_gates = jnp.concatenate([grad_out, gates], axis=1)
    inputs = gather_ring(saved_input, local_count, moves)
    rows_all = gather_ring(grads_gates, local_count, moves)
    row_grads = rows_all[:, :model_width]
    row_gates = rows_all[:, model_width:]
    first = lax.axis_index("node") * experts_here
    column = jnp.arange(128, dtype=jnp.int32)[None, :]
    contract_rows = (((0,), (0,)), ((), ()))
    contract_cols = (((1,), (1,)), ((), ()))
    gate_grads = []
    up_grads = []
    down_grads = []
    partial_value = None
    for expert in range(experts_here):
        gate = jnp.sum(
            jnp.where(column == first + expert, row_gates.astype(jnp.float32), 0.0),
            axis=1,
            keepdims=True,
        )
        gate_act = jnp.dot(inputs, gate_weight[expert], preferred_element_type=jnp.float32)
        up_act = jnp.dot(inputs, up_weight[expert], preferred_element_type=jnp.float32)
        sigmoid_val = jax.nn.sigmoid(gate_act)
        hidden = (gate * gate_act * sigmoid_val * up_act).astype(jnp.bfloat16)
        down_grads.append(
            lax.dot_general(
                hidden, row_grads, contract_rows, preferred_element_type=jnp.float32
            ).astype(jnp.bfloat16)
        )
        back_grad = gate * lax.dot_general(
            row_grads, down_weight[expert], contract_cols, preferred_element_type=jnp.float32
        )
        grad_gate_act = (
            back_grad * up_act * sigmoid_val * (1.0 + gate_act * (1.0 - sigmoid_val))
        ).astype(jnp.bfloat16)
        grad_up_act = (back_grad * gate_act * sigmoid_val).astype(jnp.bfloat16)
        gate_grads.append(
            lax.dot_general(
                inputs, grad_gate_act, contract_rows, preferred_element_type=jnp.float32
            ).astype(jnp.bfloat16)
        )
        up_grads.append(
            lax.dot_general(
                inputs, grad_up_act, contract_rows, preferred_element_type=jnp.float32
            ).astype(jnp.bfloat16)
        )
        for grad, weight in ((grad_gate_act, gate_weight), (grad_up_act, up_weight)):
            term = lax.dot_general(
                grad, weight[expert], contract_cols, preferred_element_type=jnp.float32
            )
            partial_value = term if partial_value is None else partial_value + term
    partial_value = partial_value.astype(jnp.bfloat16)
    parts = 2
    width = model_width // parts
    grad_input = jnp.concatenate(
        [
            reduce_ring(partial_value[:, i * width : (i + 1) * width], local_count, moves)
            for i in range(parts)
        ],
        axis=1,
    )
    return (grad_input, jnp.stack(gate_grads), jnp.stack(up_grads), jnp.stack(down_grads))


def solution(mesh):
    per_device = ring_per_device if mesh.shape["node"] == LIMIT else slots_per_device
    in_specs = (
        P(("rep", "node", "local"), None),
        P(("rep", "node", "local"), None),
        P("node", None, "local"),
        P("node", None, "local"),
        P("node", "local", None),
        P(("rep", "node", "local"), None),
        P(("rep", "node", "local"), None),
    )
    out_specs = (
        P(("rep", "node", "local"), None),
        P(("rep", "node"), None, "local"),
        P(("rep", "node"), None, "local"),
        P(("rep", "node"), "local", None),
    )
    return jax.shard_map(
        per_device, mesh=mesh, in_specs=in_specs, out_specs=out_specs, check_vma=False
    )
```

```python
import functools

import jax
import jax.numpy as jnp
from jax import lax
from jax.experimental import pallas as pl
from jax.experimental.pallas import tpu as pltpu
from jax.sharding import PartitionSpec as P

LIMIT = 4


gate_scale = 1.0 / 256.0


def spread_rows(source, groups, local_count):
    widened = jnp.broadcast_to(source[:, None], (groups, local_count) + source.shape[1:])
    return widened.reshape((groups * local_count,) + source.shape[1:])


def slots_per_device(grad_out, saved_input, gate_weight, up_weight, down_weight, expert_ids, gate_num):
    tokens_here = grad_out.shape[0]
    model_width = grad_out.shape[1]
    groups = lax.axis_size("node")
    local_count = lax.axis_size("local")
    experts_here = gate_weight.shape[0]
    capacity = min(tokens_here, 2 * LIMIT * tokens_here // groups)
    group_of = expert_ids // experts_here
    visits = jnp.any(
        group_of[:, :, None] == jnp.arange(groups, dtype=jnp.int32)[None, None, :], axis=1
    ).astype(jnp.int32)
    before = jnp.cumsum(visits, axis=0) - visits
    slot_hit = (before[:, :, None] == jnp.arange(capacity, dtype=jnp.int32)[None, None, :]) & (
        visits[:, :, None] == 1
    )
    select = jnp.transpose(slot_hit, (1, 2, 0)).astype(jnp.bfloat16)
    expert_hot = (
        expert_ids[:, :, None] == jnp.arange(groups * experts_here, dtype=jnp.int32)[None, None, :]
    ).astype(jnp.float32)
    gate_values = jnp.sum(
        expert_hot * (gate_num.astype(jnp.float32) * gate_scale)[:, :, None], axis=1
    )
    gate_table = gate_values.reshape(tokens_here, groups, experts_here)
    send_input = jnp.einsum(
        "gct,td->gcd", select, saved_input, preferred_element_type=jnp.float32
    ).astype(jnp.bfloat16)
    send_grad = jnp.einsum(
        "gct,td->gcd", select, grad_out, preferred_element_type=jnp.float32
    ).astype(jnp.bfloat16)
    send_gate = jnp.einsum("gct,tge->gce", select.astype(jnp.float32), gate_table).astype(
        jnp.bfloat16
    )
    got_input, got_grad, got_gate = (
        lax.all_to_all(
            spread_rows(send_input, groups, local_count),
            ("node", "local"),
            split_axis=0,
            concat_axis=0,
            tiled=True,
        ),
        lax.all_to_all(
            spread_rows(send_grad, groups, local_count),
            ("node", "local"),
            split_axis=0,
            concat_axis=0,
            tiled=True,
        ),
        lax.all_to_all(
            spread_rows(send_gate, groups, local_count),
            ("node", "local"),
            split_axis=0,
            concat_axis=0,
            tiled=True,
        ),
    )
    rows_input = got_input.reshape(groups, local_count, capacity, model_width)
    rows_grad = got_grad.reshape(groups, local_count, capacity, model_width)
    rows_gate = got_gate.reshape(groups, local_count, capacity, experts_here)
    row_count = groups * local_count * capacity
    inputs = rows_input.reshape(row_count, model_width)
    row_grads = rows_grad.reshape(row_count, model_width)
    row_gates = rows_gate.reshape(row_count, experts_here)
    contract_rows = (((0,), (0,)), ((), ()))
    contract_cols = (((1,), (1,)), ((), ()))
    gate_grads = []
    up_grads = []
    down_grads = []
    pieces = []
    columns = []
    for expert in range(experts_here):
        gate_act = jnp.dot(inputs, gate_weight[expert], preferred_element_type=jnp.float32)
        up_act = jnp.dot(inputs, up_weight[expert], preferred_element_type=jnp.float32)
        sigmoid_val = jax.nn.sigmoid(gate_act)
        hidden = (gate_act * sigmoid_val * up_act).astype(jnp.bfloat16)
        scaled = (
            row_gates[:, expert : expert + 1].astype(jnp.float32) * row_grads.astype(jnp.float32)
        ).astype(jnp.bfloat16)
        down_grads.append(
            lax.dot_general(
                hidden, scaled, contract_rows, preferred_element_type=jnp.float32
            ).astype(jnp.bfloat16)
        )
        back_grad = lax.dot_general(
            scaled, down_weight[expert], contract_cols, preferred_element_type=jnp.float32
        )
        grad_gate_act = (
            back_grad * up_act * sigmoid_val * (1.0 + gate_act * (1.0 - sigmoid_val))
        ).astype(jnp.bfloat16)
        grad_up_act = (back_grad * gate_act * sigmoid_val).astype(jnp.bfloat16)
        gate_grads.append(
            lax.dot_general(
                inputs, grad_gate_act, contract_rows, preferred_element_type=jnp.float32
            ).astype(jnp.bfloat16)
        )
        up_grads.append(
            lax.dot_general(
                inputs, grad_up_act, contract_rows, preferred_element_type=jnp.float32
            ).astype(jnp.bfloat16)
        )
        pieces.append(grad_gate_act)
        pieces.append(grad_up_act)
        columns.append(gate_weight[expert])
        columns.append(up_weight[expert])
    activations = jnp.concatenate(pieces, axis=1)
    stacked = jnp.concatenate(columns, axis=1)
    partial_value = lax.dot_general(
        activations, stacked, contract_cols, preferred_element_type=jnp.float32
    )
    returned = lax.all_to_all(
        partial_value.reshape(groups * local_count, capacity, model_width),
        ("node", "local"),
        split_axis=0,
        concat_axis=0,
        tiled=True,
    )
    group_grads = jnp.sum(
        returned.reshape(groups, local_count, capacity, model_width), axis=1
    ).astype(jnp.bfloat16)
    grad_input = jnp.einsum(
        "gct,gcd->td", select, group_grads, preferred_element_type=jnp.float32
    ).astype(jnp.bfloat16)
    return (grad_input, jnp.stack(gate_grads), jnp.stack(up_grads), jnp.stack(down_grads))


LANES = 128
STREAMS = 3
NT = (((1,), (1,)), ((), ()))
TN = (((0,), (0,)), ((), ()))
VMEM = pl.BlockSpec(memory_space=pltpu.VMEM)
ANY = pl.BlockSpec(memory_space=pl.ANY)


def ring_moves(local_count):
    ring_len = 2 * local_count

    def place(core, spot):
        spot = spot % ring_len
        if spot < local_count:
            return core * local_count + spot
        return (2 + core) * local_count + ring_len - 1 - spot

    spots = range(ring_len)
    forth = [(place(0, i), place(0, i + 1)) for i in spots]
    forth += [(place(1, i), place(1, i - 1)) for i in spots]
    back = [(there, here) for here, there in forth]
    swap = [(place(core, i), place(1 - core, i)) for i in spots for core in (0, 1)]
    partner = dict(swap)
    back_swap = [(here, partner[there]) for here, there in back]
    return forth, back, swap, back_swap


def move(value, pairs):
    return lax.ppermute(value, ("node", "local"), pairs)


def gather_ring(mine, local_count, moves):
    forth, _, swap, _ = moves
    rows = mine[0].shape[0]
    others = [move(value, swap) for value in mine]
    blocks = [jnp.concatenate(pair, axis=0) for pair in zip(mine, others, strict=True)]
    near = [[value] for value in mine]
    for _ in range(local_count - 1):
        for i, block in enumerate(blocks):
            blocks[i] = move(block, forth)
            near[i].append(blocks[i])
    for i, block in enumerate(blocks):
        near[i].append(move(block[:rows], forth))
    near = [jnp.concatenate(parts, axis=0) for parts in near]
    return [(value, move(value, swap)) for value in near]


def reduce_ring(near, far, local_count, moves, beside):
    _, back, swap, back_swap = moves
    half = near.shape[0]
    rows = half // (2 * local_count)
    wide = jnp.float32
    made = []
    from_other = move(far, swap)

    def own(start, count):
        part = slice(start, start + count)
        return near[part].astype(wide) + from_other[part].astype(wide)

    def hop(value):
        moved = move(value, back)
        if len(made) < len(beside):
            moved, result = lax.optimization_barrier((moved, beside[len(made)](value)))
            made.append(result)
        return moved

    start = half - rows
    moving = hop(own(start, rows).astype(jnp.bfloat16))
    for step in range(local_count - 1):
        start -= 2 * rows
        held = own(start, 2 * rows)
        arrived = moving.astype(wide)
        if step == 0:
            held = jnp.concatenate([held[:rows] + arrived, held[rows:]], axis=0)
        else:
            held = held + arrived
        held = held.astype(jnp.bfloat16)
        if step < local_count - 2:
            moving = hop(held)
    moving = move(held[:rows], back)
    crossed = move(held[rows:], back_swap)
    while len(made) < len(beside):
        made.append(beside[len(made)](held))
    total = own(0, rows) + moving.astype(wide) + crossed.astype(wide)
    return total.astype(jnp.bfloat16), made


def cut_columns(total, count):
    units = total // LANES
    return [i * units // count * LANES for i in range(count + 1)]


def pieces(cuts, start, stop, widest):
    found = []
    for stream in range(len(cuts) - 1):
        low, high = max(start, cuts[stream]), min(stop, cuts[stream + 1])
        if low >= high:
            continue
        count = -(-(high - low) // widest)
        marks = [low + at for at in cut_columns(high - low, count)]
        for a, b in zip(marks[:-1], marks[1:], strict=True):
            found.append((stream, a - cuts[stream], a - start, b - a))
    return found


def joined(refs, piece):
    stream, at, _, size = piece
    near, far = refs[2 * stream], refs[2 * stream + 1]
    return jnp.concatenate([near[:, at : at + size], far[:, at : at + size]], axis=0)


def prepare_kernel(cuts, inputs, grads, ids, nums, *rest):
    count = len(cuts) - 1
    outs = rest[:count]
    ids_ref, nums_ref, sem = rest[count:]
    model_width = grads.shape[1]
    copies = []

    def start(source, target):
        copy = pltpu.make_async_copy(source, target, sem.at[len(copies)])
        copy.start()
        copies.append(copy)

    start(ids, ids_ref)
    start(nums, nums_ref)
    for base, array in ((0, inputs), (model_width, grads)):
        for stream, at, offset, size in pieces(cuts, base, base + model_width, model_width):
            start(array.at[:, pl.ds(offset, size)], outs[stream].at[:, pl.ds(at, size)])
    copies[0].wait()
    copies[1].wait()
    picks, tokens_here = ids_ref.shape
    expert = lax.broadcasted_iota(jnp.int32, (LANES, tokens_here), 0)
    gates = jnp.zeros((LANES, tokens_here), jnp.float32)
    for pick in range(picks):
        value = nums_ref[pick : pick + 1, :].astype(jnp.float32) * gate_scale
        gates += jnp.where(expert == ids_ref[pick : pick + 1, :], value, 0.0)
    outs[-1][:, cuts[-1] - cuts[-2] - LANES :] = gates.T.astype(jnp.bfloat16)
    for copy in copies[2:]:
        copy.wait()


def gate_kernel(parts, *refs):
    *streams, gate_ref, act_ref = refs
    experts_here, _, width = gate_ref.shape
    for expert in range(experts_here):
        total = None
        for piece in parts:
            _, _, at, size = piece
            term = jnp.dot(
                joined(streams, piece),
                gate_ref[expert, at : at + size, :],
                preferred_element_type=jnp.float32,
            )
            total = term if total is None else total + term
        act_ref[:, expert * width : (expert + 1) * width] = total


def up_kernel(parts, *refs):
    *streams, up_ref, act_ref, hidden_ref, by_gate_ref, by_up_ref = refs
    experts_here, _, width = up_ref.shape
    for expert in range(experts_here):
        cols = slice(expert * width, (expert + 1) * width)
        up_act = None
        for piece in parts:
            _, _, at, size = piece
            term = jnp.dot(
                joined(streams, piece),
                up_ref[expert, at : at + size, :],
                preferred_element_type=jnp.float32,
            )
            up_act = term if up_act is None else up_act + term
        gate_act = act_ref[:, cols]
        sigmoid_val = jax.nn.sigmoid(gate_act)
        silu = gate_act * sigmoid_val
        hidden_ref[:, cols] = silu * up_act
        by_gate_ref[:, cols] = up_act * sigmoid_val * (1.0 + gate_act * (1.0 - sigmoid_val))
        by_up_ref[:, cols] = silu


def backward_kernel(parts, gate_part, *refs):
    *streams, hidden_ref, by_gate_ref, by_up_ref, gate_ref, up_ref, down_ref = refs[:-4]
    dnear_ref, dfar_ref, acts_ref, hidden_out_ref = refs[-4:]
    experts_here, model_width, width = gate_ref.shape
    half = dnear_ref.shape[0]
    first = lax.axis_index("node") * experts_here
    gates = joined(streams, gate_part).astype(jnp.float32)
    column = lax.broadcasted_iota(jnp.int32, gates.shape, 1)
    for expert in range(experts_here):
        cols = slice(expert * width, (expert + 1) * width)
        back_grad = None
        for piece in parts:
            _, _, at, size = piece
            term = lax.dot_general(
                joined(streams, piece),
                down_ref[expert, :, at : at + size],
                NT,
                preferred_element_type=jnp.float32,
            )
            back_grad = term if back_grad is None else back_grad + term
        gate = jnp.sum(jnp.where(column == first + expert, gates, 0.0), axis=1, keepdims=True)
        back_grad = gate * back_grad
        at = 2 * expert * width
        acts_ref[:, at : at + width] = (back_grad * by_gate_ref[:, cols]).astype(jnp.bfloat16)
        acts_ref[:, at + width : at + 2 * width] = (back_grad * by_up_ref[:, cols]).astype(
            jnp.bfloat16
        )
        hidden_out_ref[:, cols] = (gate * hidden_ref[:, cols]).astype(jnp.bfloat16)
    marks = cut_columns(model_width, 7)
    for low, high in zip(marks[:-1], marks[1:], strict=True):
        rows = slice(low, high)
        total = None
        for expert in range(experts_here):
            for k, weight in enumerate((gate_ref, up_ref)):
                at = (2 * expert + k) * width
                term = lax.dot_general(
                    acts_ref[:, at : at + width],
                    weight[expert, rows, :],
                    NT,
                    preferred_element_type=jnp.float32,
                )
                total = term if total is None else total + term
        dnear_ref[:, rows] = total[:half]
        dfar_ref[:, rows] = total[half:].astype(jnp.bfloat16)


def input_weight_kernel(k, parts, *refs):
    *streams, acts_ref, _, out_ref, staged, sem = refs
    experts_here, _, width = staged.shape
    copies = []
    for i, piece in enumerate(parts):
        _, _, at, size = piece
        turned = joined(streams, piece).T
        for expert in range(experts_here):
            first = (2 * expert + k) * width
            staged[expert, at : at + size, :] = jnp.dot(
                turned, acts_ref[:, first : first + width], preferred_element_type=jnp.float32
            ).astype(jnp.bfloat16)
            rows = pl.ds(at, size)
            copy = pltpu.make_async_copy(
                staged.at[expert, rows, :], out_ref.at[expert, rows, :], sem.at[i, expert]
            )
            copy.start()
            copies.append(copy)
    for copy in copies:
        copy.wait()


def down_weight_kernel(parts, *refs):
    *streams, hidden_ref, _, out_ref, staged, sem = refs
    experts_here, width, _ = staged.shape
    copies = []
    turned = [
        hidden_ref[:, expert * width : (expert + 1) * width].T for expert in range(experts_here)
    ]
    for i, piece in enumerate(parts):
        _, _, at, size = piece
        grads = joined(streams, piece)
        for expert in range(experts_here):
            staged[expert, :, at : at + size] = jnp.dot(
                turned[expert], grads, preferred_element_type=jnp.float32
            ).astype(jnp.bfloat16)
            cols = pl.ds(at, size)
            copy = pltpu.make_async_copy(
                staged.at[expert, :, cols], out_ref.at[expert, :, cols], sem.at[i, expert]
            )
            copy.start()
            copies.append(copy)
    for copy in copies:
        copy.wait()


def call(kernel, name, out_shape, mib, args, matmuls=0, out_specs=None, scratch=(), anys=()):
    flops = 2 * matmuls * MATMUL_SIZE
    return pl.pallas_call(
        kernel,
        in_specs=[ANY if i in anys else VMEM for i in range(len(args))],
        out_specs=out_specs or [VMEM] * len(out_shape),
        out_shape=out_shape,
        scratch_shapes=list(scratch),
        compiler_params=pltpu.CompilerParams(vmem_limit_bytes=mib << 20),
        cost_estimate=pl.CostEstimate(
            flops=flops, bytes_accessed=matmuls * MATMUL_SIZE // 64, transcendentals=0
        ),
        name=name,
    )(*args)


MATMUL_SIZE = 256 * 3584 * 256


def ring_per_device(
    grad_out, saved_input, gate_weight, up_weight, down_weight, expert_ids, gate_num
):
    tokens_here, model_width = grad_out.shape
    local_count = lax.axis_size("local")
    experts_here, _, width = gate_weight.shape
    moves = ring_moves(local_count)
    picks = expert_ids.shape[1]
    cuts = cut_columns(2 * model_width + LANES, STREAMS)

    def shaped(*shape, dtype=jnp.bfloat16):
        return jax.ShapeDtypeStruct(shape, dtype)

    mine = call(
        functools.partial(prepare_kernel, cuts),
        "prepare",
        [shaped(tokens_here, b - a) for a, b in zip(cuts[:-1], cuts[1:], strict=True)],
        4,
        (saved_input, grad_out, expert_ids.T, gate_num.T),
        scratch=[
            pltpu.VMEM((picks, tokens_here), jnp.int32),
            pltpu.VMEM((picks, tokens_here), jnp.int32),
            pltpu.SemaphoreType.DMA((2 * STREAMS + 2,)),
        ],
        anys=range(4),
    )
    gathered = gather_ring(mine, local_count, moves)
    half = gathered[0][0].shape[0]
    rows = 2 * half
    all_width = experts_here * width

    def streams_of(parts):
        used = sorted({piece[0] for piece in parts})
        arrays = [value for stream in used for value in gathered[stream]]
        return arrays, [(used.index(piece[0]), *piece[1:]) for piece in parts]

    wide = shaped(rows, all_width, dtype=jnp.float32)
    arrays, parts = streams_of(pieces(cuts, 0, model_width, model_width))
    (gate_act,) = call(
        functools.partial(gate_kernel, parts),
        "gate",
        [wide],
        10,
        (*arrays, gate_weight),
        experts_here,
    )
    hidden, by_gate, by_up = call(
        functools.partial(up_kernel, parts),
        "up",
        [wide] * 3,
        12,
        (*arrays, up_weight, gate_act),
        experts_here,
    )
    arrays, parts = streams_of(
        pieces(cuts, model_width, 2 * model_width, model_width)
        + pieces(cuts, 2 * model_width, 2 * model_width + LANES, LANES)
    )
    dnear, dfar, acts, hidden = call(
        functools.partial(backward_kernel, parts[:-1], parts[-1]),
        "backward",
        [
            shaped(half, model_width, dtype=jnp.float32),
            shaped(half, model_width),
            shaped(rows, 2 * all_width),
            shaped(rows, all_width),
        ],
        24,
        (*arrays, hidden, by_gate, by_up, gate_weight, up_weight, down_weight),
        3 * experts_here,
    )

    def weight_grad(kernel, name, start, value, shape, after):
        arrays, parts = streams_of(pieces(cuts, start, start + model_width, 1280))
        return call(
            functools.partial(kernel, parts),
            name,
            shaped(*shape),
            12,
            (*arrays, value, after),
            experts_here,
            out_specs=ANY,
            scratch=[
                pltpu.VMEM(shape, jnp.bfloat16),
                pltpu.SemaphoreType.DMA((len(parts), experts_here)),
            ],
            anys=(len(arrays) + 1,),
        )

    in_shape, out_shape = (experts_here, model_width, width), (experts_here, width, model_width)
    gate_kernel_grad = functools.partial(input_weight_kernel, 0)
    up_kernel_grad = functools.partial(input_weight_kernel, 1)
    grad_input, made = reduce_ring(
        dnear,
        dfar,
        local_count,
        moves,
        [
            lambda after: weight_grad(gate_kernel_grad, "gate_grad", 0, acts, in_shape, after),
            lambda after: weight_grad(up_kernel_grad, "up_grad", 0, acts, in_shape, after),
            lambda after: weight_grad(
                down_weight_kernel, "down_grad", model_width, hidden, out_shape, after
            ),
        ],
    )
    return (grad_input, *made)


def solution(mesh):
    per_device = ring_per_device if mesh.shape["node"] == LIMIT else slots_per_device
    in_specs = (
        P(("rep", "node", "local"), None),
        P(("rep", "node", "local"), None),
        P("node", None, "local"),
        P("node", None, "local"),
        P("node", "local", None),
        P(("rep", "node", "local"), None),
        P(("rep", "node", "local"), None),
    )
    out_specs = (
        P(("rep", "node", "local"), None),
        P(("rep", "node"), None, "local"),
        P(("rep", "node"), None, "local"),
        P(("rep", "node"), "local", None),
    )
    return jax.shard_map(
        per_device, mesh=mesh, in_specs=in_specs, out_specs=out_specs, check_vma=False
    )
```

```python
import functools

import jax
import jax.numpy as jnp
from jax import lax
from jax.experimental import pallas as pl
from jax.experimental.pallas import tpu as pltpu
from jax.sharding import PartitionSpec as P

LIMIT = 4


gate_scale = 1.0 / 256.0


def spread_rows(source, groups, local_count):
    widened = jnp.broadcast_to(source[:, None], (groups, local_count) + source.shape[1:])
    return widened.reshape((groups * local_count,) + source.shape[1:])


def slots_per_device(grad_out, saved_input, gate_weight, up_weight, down_weight, expert_ids, gate_num):
    tokens_here = grad_out.shape[0]
    model_width = grad_out.shape[1]
    groups = lax.axis_size("node")
    local_count = lax.axis_size("local")
    experts_here = gate_weight.shape[0]
    capacity = min(tokens_here, 2 * LIMIT * tokens_here // groups)
    group_of = expert_ids // experts_here
    visits = jnp.any(
        group_of[:, :, None] == jnp.arange(groups, dtype=jnp.int32)[None, None, :], axis=1
    ).astype(jnp.int32)
    before = jnp.cumsum(visits, axis=0) - visits
    slot_hit = (before[:, :, None] == jnp.arange(capacity, dtype=jnp.int32)[None, None, :]) & (
        visits[:, :, None] == 1
    )
    select = jnp.transpose(slot_hit, (1, 2, 0)).astype(jnp.bfloat16)
    expert_hot = (
        expert_ids[:, :, None] == jnp.arange(groups * experts_here, dtype=jnp.int32)[None, None, :]
    ).astype(jnp.float32)
    gate_values = jnp.sum(
        expert_hot * (gate_num.astype(jnp.float32) * gate_scale)[:, :, None], axis=1
    )
    gate_table = gate_values.reshape(tokens_here, groups, experts_here)
    send_input = jnp.einsum(
        "gct,td->gcd", select, saved_input, preferred_element_type=jnp.float32
    ).astype(jnp.bfloat16)
    send_grad = jnp.einsum(
        "gct,td->gcd", select, grad_out, preferred_element_type=jnp.float32
    ).astype(jnp.bfloat16)
    send_gate = jnp.einsum("gct,tge->gce", select.astype(jnp.float32), gate_table).astype(
        jnp.bfloat16
    )
    got_input, got_grad, got_gate = (
        lax.all_to_all(
            spread_rows(send_input, groups, local_count),
            ("node", "local"),
            split_axis=0,
            concat_axis=0,
            tiled=True,
        ),
        lax.all_to_all(
            spread_rows(send_grad, groups, local_count),
            ("node", "local"),
            split_axis=0,
            concat_axis=0,
            tiled=True,
        ),
        lax.all_to_all(
            spread_rows(send_gate, groups, local_count),
            ("node", "local"),
            split_axis=0,
            concat_axis=0,
            tiled=True,
        ),
    )
    rows_input = got_input.reshape(groups, local_count, capacity, model_width)
    rows_grad = got_grad.reshape(groups, local_count, capacity, model_width)
    rows_gate = got_gate.reshape(groups, local_count, capacity, experts_here)
    row_count = groups * local_count * capacity
    inputs = rows_input.reshape(row_count, model_width)
    row_grads = rows_grad.reshape(row_count, model_width)
    row_gates = rows_gate.reshape(row_count, experts_here)
    contract_rows = (((0,), (0,)), ((), ()))
    contract_cols = (((1,), (1,)), ((), ()))
    gate_grads = []
    up_grads = []
    down_grads = []
    pieces = []
    columns = []
    for expert in range(experts_here):
        gate_act = jnp.dot(inputs, gate_weight[expert], preferred_element_type=jnp.float32)
        up_act = jnp.dot(inputs, up_weight[expert], preferred_element_type=jnp.float32)
        sigmoid_val = jax.nn.sigmoid(gate_act)
        hidden = (gate_act * sigmoid_val * up_act).astype(jnp.bfloat16)
        scaled = (
            row_gates[:, expert : expert + 1].astype(jnp.float32) * row_grads.astype(jnp.float32)
        ).astype(jnp.bfloat16)
        down_grads.append(
            lax.dot_general(
                hidden, scaled, contract_rows, preferred_element_type=jnp.float32
            ).astype(jnp.bfloat16)
        )
        back_grad = lax.dot_general(
            scaled, down_weight[expert], contract_cols, preferred_element_type=jnp.float32
        )
        grad_gate_act = (
            back_grad * up_act * sigmoid_val * (1.0 + gate_act * (1.0 - sigmoid_val))
        ).astype(jnp.bfloat16)
        grad_up_act = (back_grad * gate_act * sigmoid_val).astype(jnp.bfloat16)
        gate_grads.append(
            lax.dot_general(
                inputs, grad_gate_act, contract_rows, preferred_element_type=jnp.float32
            ).astype(jnp.bfloat16)
        )
        up_grads.append(
            lax.dot_general(
                inputs, grad_up_act, contract_rows, preferred_element_type=jnp.float32
            ).astype(jnp.bfloat16)
        )
        pieces.append(grad_gate_act)
        pieces.append(grad_up_act)
        columns.append(gate_weight[expert])
        columns.append(up_weight[expert])
    activations = jnp.concatenate(pieces, axis=1)
    stacked = jnp.concatenate(columns, axis=1)
    partial_value = lax.dot_general(
        activations, stacked, contract_cols, preferred_element_type=jnp.float32
    )
    returned = lax.all_to_all(
        partial_value.reshape(groups * local_count, capacity, model_width),
        ("node", "local"),
        split_axis=0,
        concat_axis=0,
        tiled=True,
    )
    group_grads = jnp.sum(
        returned.reshape(groups, local_count, capacity, model_width), axis=1
    ).astype(jnp.bfloat16)
    grad_input = jnp.einsum(
        "gct,gcd->td", select, group_grads, preferred_element_type=jnp.float32
    ).astype(jnp.bfloat16)
    return (grad_input, jnp.stack(gate_grads), jnp.stack(up_grads), jnp.stack(down_grads))


LANES = 128
STREAMS = 3
NT = (((1,), (1,)), ((), ()))
TN = (((0,), (0,)), ((), ()))
VMEM = pl.BlockSpec(memory_space=pltpu.VMEM)
ANY = pl.BlockSpec(memory_space=pltpu.HBM)


def ring_moves(local_count):
    ring_len = 2 * local_count

    def place(core, spot):
        spot = spot % ring_len
        if spot < local_count:
            return core * local_count + spot
        return (2 + core) * local_count + ring_len - 1 - spot

    spots = range(ring_len)
    forth = [(place(0, i), place(0, i + 1)) for i in spots]
    forth += [(place(1, i), place(1, i - 1)) for i in spots]
    back = [(there, here) for here, there in forth]
    swap = [(place(core, i), place(1 - core, i)) for i in spots for core in (0, 1)]
    partner = dict(swap)
    back_swap = [(here, partner[there]) for here, there in back]
    onward = dict(back)
    back_two = [(here, onward[there]) for here, there in back]
    return forth, back, swap, back_swap, back_two


def move(value, pairs):
    return lax.ppermute(value, ("node", "local"), pairs)


def gather_ring(mine, cuts, local_count, moves):
    forth, _, swap, _, _ = moves
    rows = mine.shape[0]
    pair = jnp.concatenate([mine, move(mine, swap)], axis=0)
    blocks = [pair[:, a:b] for a, b in zip(cuts[:-1], cuts[1:], strict=True)]
    near = [[block[:rows]] for block in blocks]
    for _ in range(local_count - 1):
        for i, block in enumerate(blocks):
            blocks[i] = move(block, forth)
            near[i].append(blocks[i])
    for i, block in enumerate(blocks):
        near[i].append(move(block[:rows], forth))
    near = [jnp.concatenate(parts, axis=0) for parts in near]
    return [(value, move(value, swap)) for value in near]


def reduce_ring(near, far, local_count, moves, beside):
    _, back, swap, back_swap, back_two = moves
    half = near.shape[0]
    rows = half // (2 * local_count)
    wide = jnp.float32
    made = []

    def with_work(moved, source):
        if len(made) < len(beside):
            moved, result = lax.optimization_barrier((moved, beside[len(made)](source)))
            made.append(result)
        return moved

    from_other = with_work(move(far, swap), far)

    def own(start, count):
        part = slice(start, start + count)
        return near[part].astype(wide) + from_other[part].astype(wide)

    start = half - rows
    skipping = own(start, rows).astype(jnp.bfloat16)
    held = None
    for step in range(local_count - 1):
        start -= 2 * rows
        if held is None:
            held = own(start, 2 * rows)
        else:
            held = own(start, 2 * rows) + moving.astype(wide)
        if step == 1:
            held = jnp.concatenate([held[:rows] + skipped.astype(wide), held[rows:]], axis=0)
        held = held.astype(jnp.bfloat16)
        if step < local_count - 2:
            moving = move(held, back)
            if step > 0:
                moving = with_work(moving, held)
        if step == 0:
            skipped = move(skipping, back_two)
    moving = with_work(move(held[:rows], back), held)
    crossed = move(held[rows:], back_swap)
    while len(made) < len(beside):
        made.append(beside[len(made)](held))
    total = own(0, rows) + moving.astype(wide) + crossed.astype(wide)
    return total.astype(jnp.bfloat16), made


def cut_columns(total, count):
    units = total // LANES
    return [i * units // count * LANES for i in range(count + 1)]


def pieces(cuts, start, stop, widest):
    found = []
    for stream in range(len(cuts) - 1):
        low, high = max(start, cuts[stream]), min(stop, cuts[stream + 1])
        if low >= high:
            continue
        count = -(-(high - low) // widest)
        marks = [low + at for at in cut_columns(high - low, count)]
        for a, b in zip(marks[:-1], marks[1:], strict=True):
            found.append((stream, a - cuts[stream], a - start, b - a))
    return found


def joined(refs, piece):
    stream, at, _, size = piece
    near, far = refs[2 * stream], refs[2 * stream + 1]
    return jnp.concatenate([near[:, at : at + size], far[:, at : at + size]], axis=0)


def gate_kernel(parts, *refs):
    *streams, gate_ref, act_ref = refs
    experts_here, _, width = gate_ref.shape
    for expert in range(experts_here):
        total = None
        for piece in parts:
            _, _, at, size = piece
            term = jnp.dot(
                joined(streams, piece),
                gate_ref[expert, at : at + size, :],
                preferred_element_type=jnp.float32,
            )
            total = term if total is None else total + term
        act_ref[:, expert * width : (expert + 1) * width] = total


def up_kernel(parts, *refs):
    *streams, up_ref, act_ref, hidden_ref, by_gate_ref, by_up_ref = refs
    experts_here, _, width = up_ref.shape
    for expert in range(experts_here):
        cols = slice(expert * width, (expert + 1) * width)
        up_act = None
        for piece in parts:
            _, _, at, size = piece
            term = jnp.dot(
                joined(streams, piece),
                up_ref[expert, at : at + size, :],
                preferred_element_type=jnp.float32,
            )
            up_act = term if up_act is None else up_act + term
        gate_act = act_ref[:, cols]
        sigmoid_val = jax.nn.sigmoid(gate_act)
        silu = gate_act * sigmoid_val
        hidden_ref[:, cols] = silu * up_act
        by_gate_ref[:, cols] = up_act * sigmoid_val * (1.0 + gate_act * (1.0 - sigmoid_val))
        by_up_ref[:, cols] = silu


def backward_kernel(parts, gate_part, *refs):
    *streams, hidden_ref, by_gate_ref, by_up_ref, gate_ref, up_ref, down_ref = refs[:-4]
    dnear_ref, dfar_ref, acts_ref, hidden_out_ref = refs[-4:]
    experts_here, model_width, width = gate_ref.shape
    half = dnear_ref.shape[0]
    first = lax.axis_index("node") * experts_here
    gates = joined(streams, gate_part).astype(jnp.float32)
    column = lax.broadcasted_iota(jnp.int32, gates.shape, 1)
    for expert in range(experts_here):
        cols = slice(expert * width, (expert + 1) * width)
        back_grad = None
        for piece in parts:
            _, _, at, size = piece
            term = lax.dot_general(
                joined(streams, piece),
                down_ref[expert, :, at : at + size],
                NT,
                preferred_element_type=jnp.float32,
            )
            back_grad = term if back_grad is None else back_grad + term
        gate = jnp.sum(jnp.where(column == first + expert, gates, 0.0), axis=1, keepdims=True)
        back_grad = gate * back_grad
        at = 2 * expert * width
        acts_ref[:, at : at + width] = (back_grad * by_gate_ref[:, cols]).astype(jnp.bfloat16)
        acts_ref[:, at + width : at + 2 * width] = (back_grad * by_up_ref[:, cols]).astype(
            jnp.bfloat16
        )
        hidden_out_ref[:, cols] = (gate * hidden_ref[:, cols]).astype(jnp.bfloat16)
    marks = cut_columns(model_width, 7)
    for low, high in zip(marks[:-1], marks[1:], strict=True):
        rows = slice(low, high)
        total = None
        for expert in range(experts_here):
            for k, weight in enumerate((gate_ref, up_ref)):
                at = (2 * expert + k) * width
                term = lax.dot_general(
                    acts_ref[:, at : at + width],
                    weight[expert, rows, :],
                    NT,
                    preferred_element_type=jnp.float32,
                )
                total = term if total is None else total + term
        dnear_ref[:, rows] = total[:half]
        dfar_ref[:, rows] = total[half:].astype(jnp.bfloat16)


def input_weight_kernel(k, parts, *refs):
    *streams, acts_ref, _, out_ref, staged, sem = refs
    experts_here, _, width = staged.shape
    copies = []
    for i, piece in enumerate(parts):
        _, _, at, size = piece
        turned = joined(streams, piece).T
        for expert in range(experts_here):
            first = (2 * expert + k) * width
            staged[expert, at : at + size, :] = jnp.dot(
                turned, acts_ref[:, first : first + width], preferred_element_type=jnp.float32
            ).astype(jnp.bfloat16)
            rows = pl.ds(at, size)
            copy = pltpu.make_async_copy(
                staged.at[expert, rows, :], out_ref.at[expert, rows, :], sem.at[i, expert]
            )
            copy.start()
            copies.append(copy)
    for copy in copies:
        copy.wait()


def down_weight_kernel(parts, *refs):
    *streams, hidden_ref, _, out_ref, staged, sem = refs
    experts_here, width, _ = staged.shape
    copies = []
    turned = [
        hidden_ref[:, expert * width : (expert + 1) * width].T for expert in range(experts_here)
    ]
    for i, piece in enumerate(parts):
        _, _, at, size = piece
        grads = joined(streams, piece)
        for expert in range(experts_here):
            staged[expert, :, at : at + size] = jnp.dot(
                turned[expert], grads, preferred_element_type=jnp.float32
            ).astype(jnp.bfloat16)
            cols = pl.ds(at, size)
            copy = pltpu.make_async_copy(
                staged.at[expert, :, cols], out_ref.at[expert, :, cols], sem.at[i, expert]
            )
            copy.start()
            copies.append(copy)
    for copy in copies:
        copy.wait()


def call(kernel, name, out_shape, mib, args, matmuls=0, out_specs=None, scratch=(), anys=()):
    flops = 2 * matmuls * MATMUL_SIZE // 16
    return pl.pallas_call(
        kernel,
        in_specs=[ANY if i in anys else VMEM for i in range(len(args))],
        out_specs=out_specs or [VMEM] * len(out_shape),
        out_shape=out_shape,
        scratch_shapes=list(scratch),
        compiler_params=pltpu.CompilerParams(vmem_limit_bytes=mib << 20),
        cost_estimate=pl.CostEstimate(
            flops=flops, bytes_accessed=matmuls * MATMUL_SIZE // 2048, transcendentals=0
        ),
        name=name,
    )(*args)


MATMUL_SIZE = 256 * 3584 * 256


def ring_per_device(
    grad_out, saved_input, gate_weight, up_weight, down_weight, expert_ids, gate_num
):
    tokens_here, model_width = grad_out.shape
    local_count = lax.axis_size("local")
    experts_here, _, width = gate_weight.shape
    moves = ring_moves(local_count)
    cuts = cut_columns(2 * model_width + LANES, STREAMS)

    def shaped(*shape, dtype=jnp.bfloat16):
        return jax.ShapeDtypeStruct(shape, dtype)

    expert_hot = expert_ids[:, :, None] == jnp.arange(LANES, dtype=jnp.int32)[None, None, :]
    gates = jnp.sum(jnp.where(expert_hot, gate_num[:, :, None], 0), axis=1)
    gates = (gates.astype(jnp.float32) * gate_scale).astype(jnp.bfloat16)
    mine = jnp.concatenate([saved_input, grad_out, gates], axis=1)
    mine = lax.optimization_barrier(mine)
    gathered = gather_ring(mine, cuts, local_count, moves)
    half = gathered[0][0].shape[0]
    rows = 2 * half
    all_width = experts_here * width

    def streams_of(parts):
        used = sorted({piece[0] for piece in parts})
        arrays = [value for stream in used for value in gathered[stream]]
        return arrays, [(used.index(piece[0]), *piece[1:]) for piece in parts]

    wide = shaped(rows, all_width, dtype=jnp.float32)
    arrays, parts = streams_of(pieces(cuts, 0, model_width, model_width))
    (gate_act,) = call(
        functools.partial(gate_kernel, parts),
        "gate",
        [wide],
        10,
        (*arrays, gate_weight),
        experts_here,
    )
    hidden, by_gate, by_up = call(
        functools.partial(up_kernel, parts),
        "up",
        [wide] * 3,
        12,
        (*arrays, up_weight, gate_act),
        experts_here,
    )
    arrays, parts = streams_of(
        pieces(cuts, model_width, 2 * model_width, model_width)
        + pieces(cuts, 2 * model_width, 2 * model_width + LANES, LANES)
    )
    dnear, dfar, acts, hidden = call(
        functools.partial(backward_kernel, parts[:-1], parts[-1]),
        "backward",
        [
            shaped(half, model_width, dtype=jnp.float32),
            shaped(half, model_width),
            shaped(rows, 2 * all_width),
            shaped(rows, all_width),
        ],
        24,
        (*arrays, hidden, by_gate, by_up, gate_weight, up_weight, down_weight),
        3 * experts_here,
    )

    def weight_grad(kernel, name, start, value, shape, after):
        arrays, parts = streams_of(pieces(cuts, start, start + model_width, 1280))
        return call(
            functools.partial(kernel, parts),
            name,
            shaped(*shape),
            12,
            (*arrays, value, after),
            experts_here,
            out_specs=ANY,
            scratch=[
                pltpu.VMEM(shape, jnp.bfloat16),
                pltpu.SemaphoreType.DMA((len(parts), experts_here)),
            ],
            anys=(len(arrays) + 1,),
        )

    in_shape, out_shape = (experts_here, model_width, width), (experts_here, width, model_width)
    gate_kernel_grad = functools.partial(input_weight_kernel, 0)
    up_kernel_grad = functools.partial(input_weight_kernel, 1)
    grad_input, made = reduce_ring(
        dnear,
        dfar,
        local_count,
        moves,
        [
            lambda after: weight_grad(gate_kernel_grad, "gate_grad", 0, acts, in_shape, after),
            lambda after: weight_grad(up_kernel_grad, "up_grad", 0, acts, in_shape, after),
            lambda after: weight_grad(
                down_weight_kernel, "down_grad", model_width, hidden, out_shape, after
            ),
        ],
    )
    return (grad_input, *made)


def solution(mesh):
    per_device = ring_per_device if mesh.shape["node"] == LIMIT else slots_per_device
    in_specs = (
        P(("rep", "node", "local"), None),
        P(("rep", "node", "local"), None),
        P("node", None, "local"),
        P("node", None, "local"),
        P("node", "local", None),
        P(("rep", "node", "local"), None),
        P(("rep", "node", "local"), None),
    )
    out_specs = (
        P(("rep", "node", "local"), None),
        P(("rep", "node"), None, "local"),
        P(("rep", "node"), None, "local"),
        P(("rep", "node"), "local", None),
    )
    return jax.shard_map(
        per_device, mesh=mesh, in_specs=in_specs, out_specs=out_specs, check_vma=False
    )
```

```python
import functools

import jax
import jax.numpy as jnp
from jax import lax
from jax.experimental import pallas as pl
from jax.experimental.pallas import tpu as pltpu
from jax.sharding import PartitionSpec as P

LIMIT = 4


gate_scale = 1.0 / 256.0


def spread_rows(source, groups, local_count):
    widened = jnp.broadcast_to(source[:, None], (groups, local_count) + source.shape[1:])
    return widened.reshape((groups * local_count,) + source.shape[1:])


def slots_per_device(grad_out, saved_input, gate_weight, up_weight, down_weight, expert_ids, gate_num):
    tokens_here = grad_out.shape[0]
    model_width = grad_out.shape[1]
    groups = lax.axis_size("node")
    local_count = lax.axis_size("local")
    experts_here = gate_weight.shape[0]
    capacity = min(tokens_here, 2 * LIMIT * tokens_here // groups)
    group_of = expert_ids // experts_here
    visits = jnp.any(
        group_of[:, :, None] == jnp.arange(groups, dtype=jnp.int32)[None, None, :], axis=1
    ).astype(jnp.int32)
    before = jnp.cumsum(visits, axis=0) - visits
    slot_hit = (before[:, :, None] == jnp.arange(capacity, dtype=jnp.int32)[None, None, :]) & (
        visits[:, :, None] == 1
    )
    select = jnp.transpose(slot_hit, (1, 2, 0)).astype(jnp.bfloat16)
    expert_hot = (
        expert_ids[:, :, None] == jnp.arange(groups * experts_here, dtype=jnp.int32)[None, None, :]
    ).astype(jnp.float32)
    gate_values = jnp.sum(
        expert_hot * (gate_num.astype(jnp.float32) * gate_scale)[:, :, None], axis=1
    )
    gate_table = gate_values.reshape(tokens_here, groups, experts_here)
    send_input = jnp.einsum(
        "gct,td->gcd", select, saved_input, preferred_element_type=jnp.float32
    ).astype(jnp.bfloat16)
    send_grad = jnp.einsum(
        "gct,td->gcd", select, grad_out, preferred_element_type=jnp.float32
    ).astype(jnp.bfloat16)
    send_gate = jnp.einsum("gct,tge->gce", select.astype(jnp.float32), gate_table).astype(
        jnp.bfloat16
    )
    got_input, got_grad, got_gate = (
        lax.all_to_all(
            spread_rows(send_input, groups, local_count),
            ("node", "local"),
            split_axis=0,
            concat_axis=0,
            tiled=True,
        ),
        lax.all_to_all(
            spread_rows(send_grad, groups, local_count),
            ("node", "local"),
            split_axis=0,
            concat_axis=0,
            tiled=True,
        ),
        lax.all_to_all(
            spread_rows(send_gate, groups, local_count),
            ("node", "local"),
            split_axis=0,
            concat_axis=0,
            tiled=True,
        ),
    )
    rows_input = got_input.reshape(groups, local_count, capacity, model_width)
    rows_grad = got_grad.reshape(groups, local_count, capacity, model_width)
    rows_gate = got_gate.reshape(groups, local_count, capacity, experts_here)
    row_count = groups * local_count * capacity
    inputs = rows_input.reshape(row_count, model_width)
    row_grads = rows_grad.reshape(row_count, model_width)
    row_gates = rows_gate.reshape(row_count, experts_here)
    contract_rows = (((0,), (0,)), ((), ()))
    contract_cols = (((1,), (1,)), ((), ()))
    gate_grads = []
    up_grads = []
    down_grads = []
    pieces = []
    columns = []
    for expert in range(experts_here):
        gate_act = jnp.dot(inputs, gate_weight[expert], preferred_element_type=jnp.float32)
        up_act = jnp.dot(inputs, up_weight[expert], preferred_element_type=jnp.float32)
        sigmoid_val = jax.nn.sigmoid(gate_act)
        hidden = (gate_act * sigmoid_val * up_act).astype(jnp.bfloat16)
        scaled = (
            row_gates[:, expert : expert + 1].astype(jnp.float32) * row_grads.astype(jnp.float32)
        ).astype(jnp.bfloat16)
        down_grads.append(
            lax.dot_general(
                hidden, scaled, contract_rows, preferred_element_type=jnp.float32
            ).astype(jnp.bfloat16)
        )
        back_grad = lax.dot_general(
            scaled, down_weight[expert], contract_cols, preferred_element_type=jnp.float32
        )
        grad_gate_act = (
            back_grad * up_act * sigmoid_val * (1.0 + gate_act * (1.0 - sigmoid_val))
        ).astype(jnp.bfloat16)
        grad_up_act = (back_grad * gate_act * sigmoid_val).astype(jnp.bfloat16)
        gate_grads.append(
            lax.dot_general(
                inputs, grad_gate_act, contract_rows, preferred_element_type=jnp.float32
            ).astype(jnp.bfloat16)
        )
        up_grads.append(
            lax.dot_general(
                inputs, grad_up_act, contract_rows, preferred_element_type=jnp.float32
            ).astype(jnp.bfloat16)
        )
        pieces.append(grad_gate_act)
        pieces.append(grad_up_act)
        columns.append(gate_weight[expert])
        columns.append(up_weight[expert])
    activations = jnp.concatenate(pieces, axis=1)
    stacked = jnp.concatenate(columns, axis=1)
    partial_value = lax.dot_general(
        activations, stacked, contract_cols, preferred_element_type=jnp.float32
    )
    returned = lax.all_to_all(
        partial_value.reshape(groups * local_count, capacity, model_width),
        ("node", "local"),
        split_axis=0,
        concat_axis=0,
        tiled=True,
    )
    group_grads = jnp.sum(
        returned.reshape(groups, local_count, capacity, model_width), axis=1
    ).astype(jnp.bfloat16)
    grad_input = jnp.einsum(
        "gct,gcd->td", select, group_grads, preferred_element_type=jnp.float32
    ).astype(jnp.bfloat16)
    return (grad_input, jnp.stack(gate_grads), jnp.stack(up_grads), jnp.stack(down_grads))


LANES = 128
STREAMS = 3
NT = (((1,), (1,)), ((), ()))
TN = (((0,), (0,)), ((), ()))
VMEM = pl.BlockSpec(memory_space=pltpu.VMEM)
ANY = pl.BlockSpec(memory_space=pltpu.HBM)


def ring_moves(local_count):
    ring_len = 2 * local_count

    def place(core, spot):
        spot = spot % ring_len
        if spot < local_count:
            return core * local_count + spot
        return (2 + core) * local_count + ring_len - 1 - spot

    spots = range(ring_len)
    forth = [(place(0, i), place(0, i + 1)) for i in spots]
    forth += [(place(1, i), place(1, i - 1)) for i in spots]
    back = [(there, here) for here, there in forth]
    swap = [(place(core, i), place(1 - core, i)) for i in spots for core in (0, 1)]
    partner = dict(swap)
    back_swap = [(here, partner[there]) for here, there in back]
    backs = [
        [(place(core, i), place(core, i + (2 * core - 1) * hops)) for i in spots for core in (0, 1)]
        for hops in range(local_count)
    ]
    return forth, backs, swap, back_swap


def move(value, pairs):
    return lax.ppermute(value, ("node", "local"), pairs)


def gather_ring(mine, gates, cuts, local_count, moves):
    forth, _, swap, _ = moves
    rows = mine.shape[0]
    pair = jnp.concatenate([mine, move(mine, swap)], axis=0)
    gates = jnp.concatenate([gates, move(gates, swap)], axis=0)
    blocks = [pair[:, a:b] for a, b in zip(cuts[:-1], cuts[1:], strict=True)]
    blocks[-1] = jnp.concatenate([blocks[-1], gates], axis=1)
    near = [[block[:rows]] for block in blocks]
    for _ in range(local_count - 1):
        for i, block in enumerate(blocks):
            blocks[i] = move(block, forth)
            near[i].append(blocks[i])
    for i, block in enumerate(blocks):
        near[i].append(move(block[:rows], forth))
    near = [jnp.concatenate(parts, axis=0) for parts in near]
    return [(value, move(value, swap)) for value in near]


def reduce_ring(near, far, local_count, moves, beside):
    _, backs, swap, back_swap = moves
    half = near[0].shape[0]
    rows = half // (2 * local_count)
    wide = jnp.float32
    made = []

    def with_work(moved, source):
        if len(made) < len(beside):
            moved, result = lax.optimization_barrier((moved, beside[len(made)](source)))
            made.append(result)
        return moved

    from_other = [move(value, swap) for value in far]

    def part(column, start, count):
        rows_here = slice(start, start + count)
        return near[column][rows_here].astype(wide) + from_other[column][rows_here].astype(wide)

    def own(start, count):
        return jnp.concatenate([part(i, start, count) for i in range(len(near))], axis=1)

    blocks = [own((2 * hops - 1) * rows, 2 * rows) for hops in range(1, local_count)]
    blocks.append(own(half - rows, rows))
    sent = [block.astype(jnp.bfloat16) for block in blocks]
    moved = []
    for hops, value in enumerate(sent):
        if hops == 2:
            early = [
                part(i, (2 * hops + 1) * rows, 2 * rows).astype(jnp.bfloat16)
                for i in range(len(near))
            ]
            value = jnp.concatenate([move(piece, backs[hops]) for piece in early], axis=1)
            moved.append(value)
        elif hops:
            moved.append(move(value, backs[hops]))
    for i in range(min(2, len(moved))):
        moved[i] = with_work(moved[i], sent[1])
    held = blocks[0]
    for value in moved[:-1]:
        held = held + value.astype(wide)
    held = jnp.concatenate([held[:rows] + moved[-1].astype(wide), held[rows:]], axis=0)
    held = held.astype(jnp.bfloat16)
    moving = with_work(move(held[:rows], backs[1]), held)
    crossed = move(held[rows:], back_swap)
    while len(made) < len(beside):
        made.append(beside[len(made)](held))
    total = own(0, rows) + moving.astype(wide) + crossed.astype(wide)
    return total.astype(jnp.bfloat16), made


def cut_columns(total, count):
    units = total // LANES
    return [i * units // count * LANES for i in range(count + 1)]


def pieces(cuts, start, stop, widest):
    found = []
    for stream in range(len(cuts) - 1):
        low, high = max(start, cuts[stream]), min(stop, cuts[stream + 1])
        if low >= high:
            continue
        count = -(-(high - low) // widest)
        marks = [low + at for at in cut_columns(high - low, count)]
        for a, b in zip(marks[:-1], marks[1:], strict=True):
            found.append((stream, a - cuts[stream], a - start, b - a))
    return found


def joined(refs, piece):
    stream, at, _, size = piece
    near, far = refs[2 * stream], refs[2 * stream + 1]
    return jnp.concatenate([near[:, at : at + size], far[:, at : at + size]], axis=0)


def products(parts, streams, weight_ref, expert):
    total = None
    for piece in parts:
        _, _, at, size = piece
        term = jnp.dot(
            joined(streams, piece),
            weight_ref[expert, at : at + size, :],
            preferred_element_type=jnp.float32,
        )
        total = term if total is None else total + term
    return total


def begin_kernel(parts, *refs):
    *streams, gate_ref, gate_sum_ref = refs
    experts_here, _, width = gate_ref.shape
    for expert in range(experts_here):
        cols = slice(expert * width, (expert + 1) * width)
        gate_sum_ref[:, cols] = products(parts, streams, gate_ref, expert)


def finish_kernel(parts, count, *refs):
    *streams, gate_ref, up_ref, gate_sum_ref = refs[:-3]
    hidden_ref, by_gate_ref, by_up_ref = refs[-3:]
    experts_here, _, width = up_ref.shape
    for expert in range(experts_here):
        cols = slice(expert * width, (expert + 1) * width)
        gate_act = gate_sum_ref[:, cols] + products(parts[count:], streams, gate_ref, expert)
        up_act = products(parts, streams, up_ref, expert)
        sigmoid_val = jax.nn.sigmoid(gate_act)
        silu = gate_act * sigmoid_val
        hidden_ref[:, cols] = silu * up_act
        by_gate_ref[:, cols] = up_act * sigmoid_val * (1.0 + gate_act * (1.0 - sigmoid_val))
        by_up_ref[:, cols] = silu


def backward_kernel(parts, gate_part, *refs):
    *streams, hidden_ref, by_gate_ref, by_up_ref, gate_ref, up_ref, down_ref = refs[:-4]
    dnear_ref, dfar_ref, acts_ref, hidden_out_ref = refs[-4:]
    experts_here, _, width = gate_ref.shape
    first = lax.axis_index("node") * experts_here
    gates = joined(streams, gate_part).astype(jnp.float32)
    column = lax.broadcasted_iota(jnp.int32, gates.shape, 1)
    for expert in range(experts_here):
        cols = slice(expert * width, (expert + 1) * width)
        back_grad = None
        for piece in parts:
            _, _, at, size = piece
            term = lax.dot_general(
                joined(streams, piece),
                down_ref[expert, :, at : at + size],
                NT,
                preferred_element_type=jnp.float32,
            )
            back_grad = term if back_grad is None else back_grad + term
        gate = jnp.sum(jnp.where(column == first + expert, gates, 0.0), axis=1, keepdims=True)
        back_grad = gate * back_grad
        at = 2 * expert * width
        acts_ref[:, at : at + width] = (back_grad * by_gate_ref[:, cols]).astype(jnp.bfloat16)
        acts_ref[:, at + width : at + 2 * width] = (back_grad * by_up_ref[:, cols]).astype(
            jnp.bfloat16
        )
        hidden_out_ref[:, cols] = (gate * hidden_ref[:, cols]).astype(jnp.bfloat16)
    spread(acts_ref, gate_ref, up_ref, dnear_ref, dfar_ref, 0)


def spread(acts_ref, gate_ref, up_ref, dnear_ref, dfar_ref, first):
    experts_here, _, width = gate_ref.shape
    half, span = dnear_ref.shape
    marks = cut_columns(span, -(-span // 512))
    for low, high in zip(marks[:-1], marks[1:], strict=True):
        total = None
        for expert in range(experts_here):
            for k, weight in enumerate((gate_ref, up_ref)):
                at = (2 * expert + k) * width
                term = lax.dot_general(
                    acts_ref[:, at : at + width],
                    weight[expert, first + low : first + high, :],
                    NT,
                    preferred_element_type=jnp.float32,
                )
                total = term if total is None else total + term
        dnear_ref[:, low:high] = total[:half]
        dfar_ref[:, low:high] = total[half:].astype(jnp.bfloat16)


def spread_kernel(first, acts_ref, gate_ref, up_ref, dnear_ref, dfar_ref):
    spread(acts_ref, gate_ref, up_ref, dnear_ref, dfar_ref, first)


def input_weight_kernel(k, parts, *refs):
    *streams, acts_ref, _, out_ref, staged, sem = refs
    experts_here, _, width = staged.shape
    copies = []
    for i, piece in enumerate(parts):
        _, _, at, size = piece
        turned = joined(streams, piece).T
        for expert in range(experts_here):
            first = (2 * expert + k) * width
            staged[expert, at : at + size, :] = jnp.dot(
                turned, acts_ref[:, first : first + width], preferred_element_type=jnp.float32
            ).astype(jnp.bfloat16)
            rows = pl.ds(at, size)
            copy = pltpu.make_async_copy(
                staged.at[expert, rows, :], out_ref.at[expert, rows, :], sem.at[i, expert]
            )
            copy.start()
            copies.append(copy)
    for copy in copies:
        copy.wait()


def down_weight_kernel(parts, *refs):
    *streams, hidden_ref, _, out_ref, staged, sem = refs
    experts_here, width, _ = staged.shape
    copies = []
    turned = [
        hidden_ref[:, expert * width : (expert + 1) * width].T for expert in range(experts_here)
    ]
    for i, piece in enumerate(parts):
        _, _, at, size = piece
        grads = joined(streams, piece)
        for expert in range(experts_here):
            staged[expert, :, at : at + size] = jnp.dot(
                turned[expert], grads, preferred_element_type=jnp.float32
            ).astype(jnp.bfloat16)
            cols = pl.ds(at, size)
            copy = pltpu.make_async_copy(
                staged.at[expert, :, cols], out_ref.at[expert, :, cols], sem.at[i, expert]
            )
            copy.start()
            copies.append(copy)
    for copy in copies:
        copy.wait()


def call(kernel, name, out_shape, mib, args, matmuls=0, out_specs=None, scratch=(), anys=()):
    flops = 2 * matmuls * MATMUL_SIZE
    return pl.pallas_call(
        kernel,
        in_specs=[ANY if i in anys else VMEM for i in range(len(args))],
        out_specs=out_specs or [VMEM] * len(out_shape),
        out_shape=out_shape,
        scratch_shapes=list(scratch),
        compiler_params=pltpu.CompilerParams(vmem_limit_bytes=mib << 20),
        cost_estimate=pl.CostEstimate(
            flops=flops, bytes_accessed=matmuls * MATMUL_SIZE // 128, transcendentals=0
        ),
        name=name,
    )(*args)


MATMUL_SIZE = 256 * 3584 * 256


def ring_per_device(
    grad_out, saved_input, gate_weight, up_weight, down_weight, expert_ids, gate_num
):
    tokens_here, model_width = grad_out.shape
    local_count = lax.axis_size("local")
    experts_here, _, width = gate_weight.shape
    moves = ring_moves(local_count)
    cuts = cut_columns(2 * model_width + LANES, STREAMS)

    def shaped(*shape, dtype=jnp.bfloat16):
        return jax.ShapeDtypeStruct(shape, dtype)

    mine = lax.optimization_barrier(jnp.concatenate([saved_input, grad_out], axis=1))
    _, expert_ids = lax.optimization_barrier((mine, expert_ids))
    expert_hot = expert_ids[:, :, None] == jnp.arange(LANES, dtype=jnp.int32)[None, None, :]
    gates = jnp.sum(jnp.where(expert_hot, gate_num[:, :, None], 0), axis=1)
    gates = (gates.astype(jnp.float32) * gate_scale).astype(jnp.bfloat16)
    gathered = gather_ring(mine, gates, cuts, local_count, moves)
    half = gathered[0][0].shape[0]
    rows = 2 * half
    all_width = experts_here * width

    def streams_of(parts):
        used = sorted({piece[0] for piece in parts})
        arrays = [value for stream in used for value in gathered[stream]]
        return arrays, [(used.index(piece[0]), *piece[1:]) for piece in parts]

    wide = shaped(rows, all_width, dtype=jnp.float32)
    in_parts = pieces(cuts, 0, model_width, model_width)
    arrays, parts = streams_of(in_parts[:1])
    sums = call(
        functools.partial(begin_kernel, parts),
        "begin",
        [wide],
        14,
        (*arrays, gate_weight),
        experts_here,
    )
    arrays, parts = streams_of(in_parts)
    hidden, by_gate, by_up = call(
        functools.partial(finish_kernel, parts, 1),
        "finish",
        [wide] * 3,
        16,
        (*arrays, gate_weight, up_weight, *sums),
        3 * experts_here,
    )
    arrays, parts = streams_of(
        pieces(cuts, model_width, 2 * model_width, model_width)
        + pieces(cuts, 2 * model_width, 2 * model_width + LANES, LANES)
    )
    span = cut_columns(model_width, 2)[1]
    dnear, dfar, acts, hidden = call(
        functools.partial(backward_kernel, parts[:-1], parts[-1]),
        "backward",
        [
            shaped(half, span, dtype=jnp.float32),
            shaped(half, span),
            shaped(rows, 2 * all_width),
            shaped(rows, all_width),
        ],
        24,
        (*arrays, hidden, by_gate, by_up, gate_weight, up_weight, down_weight),
        2 * experts_here,
    )
    more_near, more_far = call(
        functools.partial(spread_kernel, span),
        "spread",
        [
            shaped(half, model_width - span, dtype=jnp.float32),
            shaped(half, model_width - span),
        ],
        16,
        (acts, gate_weight, up_weight),
        experts_here,
    )

    def weight_grad(kernel, name, start, value, shape, after):
        arrays, parts = streams_of(pieces(cuts, start, start + model_width, 1280))
        return call(
            functools.partial(kernel, parts),
            name,
            shaped(*shape),
            12,
            (*arrays, value, after),
            experts_here,
            out_specs=ANY,
            scratch=[
                pltpu.VMEM(shape, jnp.bfloat16),
                pltpu.SemaphoreType.DMA((len(parts), experts_here)),
            ],
            anys=(len(arrays) + 1,),
        )

    in_shape, out_shape = (experts_here, model_width, width), (experts_here, width, model_width)
    gate_kernel_grad = functools.partial(input_weight_kernel, 0)
    up_kernel_grad = functools.partial(input_weight_kernel, 1)
    grad_input, made = reduce_ring(
        (dnear, more_near),
        (dfar, more_far),
        local_count,
        moves,
        [
            lambda after: weight_grad(gate_kernel_grad, "gate_grad", 0, acts, in_shape, after),
            lambda after: weight_grad(up_kernel_grad, "up_grad", 0, acts, in_shape, after),
            lambda after: weight_grad(
                down_weight_kernel, "down_grad", model_width, hidden, out_shape, after
            ),
        ],
    )
    return (grad_input, *made)


def solution(mesh):
    per_device = ring_per_device if mesh.shape["node"] == LIMIT else slots_per_device
    in_specs = (
        P(("rep", "node", "local"), None),
        P(("rep", "node", "local"), None),
        P("node", None, "local"),
        P("node", None, "local"),
        P("node", "local", None),
        P(("rep", "node", "local"), None),
        P(("rep", "node", "local"), None),
    )
    out_specs = (
        P(("rep", "node", "local"), None),
        P(("rep", "node"), None, "local"),
        P(("rep", "node"), None, "local"),
        P(("rep", "node"), "local", None),
    )
    return jax.shard_map(
        per_device, mesh=mesh, in_specs=in_specs, out_specs=out_specs, check_vma=False
    )
```

```python
import functools

import jax
import jax.numpy as jnp
from jax import lax
from jax.experimental import pallas as pl
from jax.experimental.pallas import tpu as pltpu
from jax.sharding import PartitionSpec as P

LIMIT = 4


gate_scale = 1.0 / 256.0


def spread_rows(source, groups, local_count):
    widened = jnp.broadcast_to(source[:, None], (groups, local_count) + source.shape[1:])
    return widened.reshape((groups * local_count,) + source.shape[1:])


def slots_per_device(grad_out, saved_input, gate_weight, up_weight, down_weight, expert_ids, gate_num):
    tokens_here = grad_out.shape[0]
    model_width = grad_out.shape[1]
    groups = lax.axis_size("node")
    local_count = lax.axis_size("local")
    experts_here = gate_weight.shape[0]
    capacity = min(tokens_here, 2 * LIMIT * tokens_here // groups)
    group_of = expert_ids // experts_here
    visits = jnp.any(
        group_of[:, :, None] == jnp.arange(groups, dtype=jnp.int32)[None, None, :], axis=1
    ).astype(jnp.int32)
    before = jnp.cumsum(visits, axis=0) - visits
    slot_hit = (before[:, :, None] == jnp.arange(capacity, dtype=jnp.int32)[None, None, :]) & (
        visits[:, :, None] == 1
    )
    select = jnp.transpose(slot_hit, (1, 2, 0)).astype(jnp.bfloat16)
    expert_hot = (
        expert_ids[:, :, None] == jnp.arange(groups * experts_here, dtype=jnp.int32)[None, None, :]
    ).astype(jnp.float32)
    gate_values = jnp.sum(
        expert_hot * (gate_num.astype(jnp.float32) * gate_scale)[:, :, None], axis=1
    )
    gate_table = gate_values.reshape(tokens_here, groups, experts_here)
    send_input = jnp.einsum(
        "gct,td->gcd", select, saved_input, preferred_element_type=jnp.float32
    ).astype(jnp.bfloat16)
    send_grad = jnp.einsum(
        "gct,td->gcd", select, grad_out, preferred_element_type=jnp.float32
    ).astype(jnp.bfloat16)
    send_gate = jnp.einsum("gct,tge->gce", select.astype(jnp.float32), gate_table).astype(
        jnp.bfloat16
    )
    got_input, got_grad, got_gate = (
        lax.all_to_all(
            spread_rows(send_input, groups, local_count),
            ("node", "local"),
            split_axis=0,
            concat_axis=0,
            tiled=True,
        ),
        lax.all_to_all(
            spread_rows(send_grad, groups, local_count),
            ("node", "local"),
            split_axis=0,
            concat_axis=0,
            tiled=True,
        ),
        lax.all_to_all(
            spread_rows(send_gate, groups, local_count),
            ("node", "local"),
            split_axis=0,
            concat_axis=0,
            tiled=True,
        ),
    )
    rows_input = got_input.reshape(groups, local_count, capacity, model_width)
    rows_grad = got_grad.reshape(groups, local_count, capacity, model_width)
    rows_gate = got_gate.reshape(groups, local_count, capacity, experts_here)
    row_count = groups * local_count * capacity
    inputs = rows_input.reshape(row_count, model_width)
    row_grads = rows_grad.reshape(row_count, model_width)
    row_gates = rows_gate.reshape(row_count, experts_here)
    contract_rows = (((0,), (0,)), ((), ()))
    contract_cols = (((1,), (1,)), ((), ()))
    gate_grads = []
    up_grads = []
    down_grads = []
    pieces = []
    columns = []
    for expert in range(experts_here):
        gate_act = jnp.dot(inputs, gate_weight[expert], preferred_element_type=jnp.float32)
        up_act = jnp.dot(inputs, up_weight[expert], preferred_element_type=jnp.float32)
        sigmoid_val = jax.nn.sigmoid(gate_act)
        hidden = (gate_act * sigmoid_val * up_act).astype(jnp.bfloat16)
        scaled = (
            row_gates[:, expert : expert + 1].astype(jnp.float32) * row_grads.astype(jnp.float32)
        ).astype(jnp.bfloat16)
        down_grads.append(
            lax.dot_general(
                hidden, scaled, contract_rows, preferred_element_type=jnp.float32
            ).astype(jnp.bfloat16)
        )
        back_grad = lax.dot_general(
            scaled, down_weight[expert], contract_cols, preferred_element_type=jnp.float32
        )
        grad_gate_act = (
            back_grad * up_act * sigmoid_val * (1.0 + gate_act * (1.0 - sigmoid_val))
        ).astype(jnp.bfloat16)
        grad_up_act = (back_grad * gate_act * sigmoid_val).astype(jnp.bfloat16)
        gate_grads.append(
            lax.dot_general(
                inputs, grad_gate_act, contract_rows, preferred_element_type=jnp.float32
            ).astype(jnp.bfloat16)
        )
        up_grads.append(
            lax.dot_general(
                inputs, grad_up_act, contract_rows, preferred_element_type=jnp.float32
            ).astype(jnp.bfloat16)
        )
        pieces.append(grad_gate_act)
        pieces.append(grad_up_act)
        columns.append(gate_weight[expert])
        columns.append(up_weight[expert])
    activations = jnp.concatenate(pieces, axis=1)
    stacked = jnp.concatenate(columns, axis=1)
    partial_value = lax.dot_general(
        activations, stacked, contract_cols, preferred_element_type=jnp.float32
    )
    returned = lax.all_to_all(
        partial_value.reshape(groups * local_count, capacity, model_width),
        ("node", "local"),
        split_axis=0,
        concat_axis=0,
        tiled=True,
    )
    group_grads = jnp.sum(
        returned.reshape(groups, local_count, capacity, model_width), axis=1
    ).astype(jnp.bfloat16)
    grad_input = jnp.einsum(
        "gct,gcd->td", select, group_grads, preferred_element_type=jnp.float32
    ).astype(jnp.bfloat16)
    return (grad_input, jnp.stack(gate_grads), jnp.stack(up_grads), jnp.stack(down_grads))


LANES = 128
STREAMS = 3
NT = (((1,), (1,)), ((), ()))
TN = (((0,), (0,)), ((), ()))
VMEM = pl.BlockSpec(memory_space=pltpu.VMEM)
ANY = pl.BlockSpec(memory_space=pltpu.HBM)


def ring_moves(local_count):
    ring_len = 2 * local_count

    def place(core, spot):
        spot = spot % ring_len
        if spot < local_count:
            return core * local_count + spot
        return (2 + core) * local_count + ring_len - 1 - spot

    spots = range(ring_len)
    forth = [(place(0, i), place(0, i + 1)) for i in spots]
    forth += [(place(1, i), place(1, i - 1)) for i in spots]
    swap = [(place(core, i), place(1 - core, i)) for i in spots for core in (0, 1)]
    partner = dict(swap)
    back_swap = [(there, partner[here]) for here, there in forth]
    backs = [
        [(place(core, i), place(core, i + (2 * core - 1) * hops)) for i in spots for core in (0, 1)]
        for hops in range(local_count)
    ]
    return forth, backs, swap, back_swap


def move(value, pairs):
    return lax.ppermute(value, ("node", "local"), pairs)


def gather_ring(mine, gates, cuts, local_count, moves):
    forth, _, swap, _ = moves
    rows = mine.shape[0]
    pair = jnp.concatenate([mine, move(mine, swap)], axis=0)
    gates = jnp.concatenate([gates, move(gates, swap)], axis=0)
    blocks = [pair[:, a:b] for a, b in zip(cuts[:-1], cuts[1:], strict=True)]
    blocks[-1] = jnp.concatenate([blocks[-1], gates], axis=1)
    near = [[block[:rows]] for block in blocks]
    for _ in range(local_count - 1):
        for i, block in enumerate(blocks):
            blocks[i] = move(block, forth)
            near[i].append(blocks[i])
    for i, block in enumerate(blocks):
        near[i].append(move(block[:rows], forth))
    near = [jnp.concatenate(parts, axis=0) for parts in near]
    return [(value, move(value, swap)) for value in near]


def reduce_ring(near, far, local_count, moves, beside):
    _, backs, swap, back_swap = moves
    half = near[0].shape[0]
    rows = half // (2 * local_count)
    wide = jnp.float32
    made = []

    def with_work(moved, source):
        if len(made) < len(beside):
            moved, result = lax.optimization_barrier((moved, beside[len(made)](source)))
            made.append(result)
        return moved

    from_other = [move(value, swap) for value in far]

    def part(column, start, count):
        rows_here = slice(start, start + count)
        return near[column][rows_here].astype(wide) + from_other[column][rows_here].astype(wide)

    def own(start, count):
        return jnp.concatenate([part(i, start, count) for i in range(len(near))], axis=1)

    blocks = [own((2 * hops - 1) * rows, 2 * rows) for hops in range(1, local_count)]
    blocks.append(own(half - rows, rows))
    sent = [block.astype(jnp.bfloat16) for block in blocks]
    moved = []
    for hops, value in enumerate(sent):
        if hops == 2:
            early = [
                part(i, (2 * hops + 1) * rows, 2 * rows).astype(jnp.bfloat16)
                for i in range(len(near))
            ]
            value = jnp.concatenate([move(piece, backs[hops]) for piece in early], axis=1)
            moved.append(value)
        elif hops:
            moved.append(move(value, backs[hops]))
    moved[0] = with_work(moved[0], sent[1])
    held = blocks[0]
    for value in moved[:-1]:
        held = held + value.astype(wide)
    held = jnp.concatenate([held[:rows] + moved[-1].astype(wide), held[rows:]], axis=0)
    held = held.astype(jnp.bfloat16)
    moving = with_work(move(held[:rows], backs[1]), held)
    crossed = move(held[rows:], back_swap)
    while len(made) < len(beside):
        made.append(beside[len(made)](held))
    total = own(0, rows) + moving.astype(wide) + crossed.astype(wide)
    return total.astype(jnp.bfloat16), made


def cut_columns(total, count):
    units = total // LANES
    return [i * units // count * LANES for i in range(count + 1)]


def pieces(cuts, start, stop, widest):
    found = []
    for stream in range(len(cuts) - 1):
        low, high = max(start, cuts[stream]), min(stop, cuts[stream + 1])
        if low >= high:
            continue
        count = -(-(high - low) // widest)
        marks = [low + at for at in cut_columns(high - low, count)]
        for a, b in zip(marks[:-1], marks[1:], strict=True):
            found.append((stream, a - cuts[stream], a - start, b - a))
    return found


def joined(refs, piece):
    stream, at, _, size = piece
    near, far = refs[2 * stream], refs[2 * stream + 1]
    return jnp.concatenate([near[:, at : at + size], far[:, at : at + size]], axis=0)


def products(parts, streams, weight_ref, expert):
    total = None
    for piece in parts:
        _, _, at, size = piece
        term = jnp.dot(
            joined(streams, piece),
            weight_ref[expert, at : at + size, :],
            preferred_element_type=jnp.float32,
        )
        total = term if total is None else total + term
    return total


def begin_kernel(parts, *refs):
    *streams, gate_ref, gate_sum_ref = refs
    experts_here, _, width = gate_ref.shape
    for expert in range(experts_here):
        cols = slice(expert * width, (expert + 1) * width)
        gate_sum_ref[:, cols] = products(parts, streams, gate_ref, expert)


def finish_kernel(parts, count, *refs):
    *streams, gate_ref, up_ref, gate_sum_ref = refs[:-3]
    hidden_ref, by_gate_ref, by_up_ref = refs[-3:]
    experts_here, _, width = up_ref.shape
    for expert in range(experts_here):
        cols = slice(expert * width, (expert + 1) * width)
        gate_act = gate_sum_ref[:, cols] + products(parts[count:], streams, gate_ref, expert)
        up_act = products(parts, streams, up_ref, expert)
        sigmoid_val = jax.nn.sigmoid(gate_act)
        silu = gate_act * sigmoid_val
        hidden_ref[:, cols] = silu * up_act
        by_gate_ref[:, cols] = up_act * sigmoid_val * (1.0 + gate_act * (1.0 - sigmoid_val))
        by_up_ref[:, cols] = silu


def backward_kernel(parts, gate_part, *refs):
    *streams, hidden_ref, by_gate_ref, by_up_ref, gate_ref, up_ref, down_ref = refs[:-4]
    dnear_ref, dfar_ref, acts_ref, hidden_out_ref = refs[-4:]
    experts_here, _, width = gate_ref.shape
    first = lax.axis_index("node") * experts_here
    gates = joined(streams, gate_part).astype(jnp.float32)
    column = lax.broadcasted_iota(jnp.int32, gates.shape, 1)
    for expert in range(experts_here):
        cols = slice(expert * width, (expert + 1) * width)
        back_grad = None
        for piece in parts:
            _, _, at, size = piece
            term = lax.dot_general(
                joined(streams, piece),
                down_ref[expert, :, at : at + size],
                NT,
                preferred_element_type=jnp.float32,
            )
            back_grad = term if back_grad is None else back_grad + term
        gate = jnp.sum(jnp.where(column == first + expert, gates, 0.0), axis=1, keepdims=True)
        back_grad = gate * back_grad
        at = 2 * expert * width
        acts_ref[:, at : at + width] = (back_grad * by_gate_ref[:, cols]).astype(jnp.bfloat16)
        acts_ref[:, at + width : at + 2 * width] = (back_grad * by_up_ref[:, cols]).astype(
            jnp.bfloat16
        )
        hidden_out_ref[:, cols] = (gate * hidden_ref[:, cols]).astype(jnp.bfloat16)
    spread(acts_ref, gate_ref, up_ref, dnear_ref, dfar_ref, 0)


def spread(acts_ref, gate_ref, up_ref, dnear_ref, dfar_ref, first):
    experts_here, _, width = gate_ref.shape
    half, span = dnear_ref.shape
    marks = cut_columns(span, -(-span // 512))
    for low, high in zip(marks[:-1], marks[1:], strict=True):
        total = None
        for expert in range(experts_here):
            for k, weight in enumerate((gate_ref, up_ref)):
                at = (2 * expert + k) * width
                term = lax.dot_general(
                    acts_ref[:, at : at + width],
                    weight[expert, first + low : first + high, :],
                    NT,
                    preferred_element_type=jnp.float32,
                )
                total = term if total is None else total + term
        dnear_ref[:, low:high] = total[:half]
        dfar_ref[:, low:high] = total[half:].astype(jnp.bfloat16)


def spread_kernel(first, acts_ref, gate_ref, up_ref, dnear_ref, dfar_ref):
    spread(acts_ref, gate_ref, up_ref, dnear_ref, dfar_ref, first)


def input_weight_kernel(parts, *refs):
    *streams, acts_ref, _, gate_out_ref, up_out_ref, staged, sem = refs
    _, experts_here, _, width = staged.shape
    copies = []
    for i, piece in enumerate(parts):
        _, _, at, size = piece
        turned = joined(streams, piece).T
        for expert in range(experts_here):
            for k, out_ref in enumerate((gate_out_ref, up_out_ref)):
                first = (2 * expert + k) * width
                staged[k, expert, at : at + size, :] = jnp.dot(
                    turned, acts_ref[:, first : first + width], preferred_element_type=jnp.float32
                ).astype(jnp.bfloat16)
                rows = pl.ds(at, size)
                copy = pltpu.make_async_copy(
                    staged.at[k, expert, rows, :], out_ref.at[expert, rows, :], sem.at[i, expert, k]
                )
                copy.start()
                copies.append(copy)
    for copy in copies:
        copy.wait()


def down_weight_kernel(parts, *refs):
    *streams, hidden_ref, _, out_ref, staged, sem = refs
    experts_here, width, _ = staged.shape
    copies = []
    turned = [
        hidden_ref[:, expert * width : (expert + 1) * width].T for expert in range(experts_here)
    ]
    for i, piece in enumerate(parts):
        _, _, at, size = piece
        grads = joined(streams, piece)
        for expert in range(experts_here):
            staged[expert, :, at : at + size] = jnp.dot(
                turned[expert], grads, preferred_element_type=jnp.float32
            ).astype(jnp.bfloat16)
            cols = pl.ds(at, size)
            copy = pltpu.make_async_copy(
                staged.at[expert, :, cols], out_ref.at[expert, :, cols], sem.at[i, expert, 0]
            )
            copy.start()
            copies.append(copy)
    for copy in copies:
        copy.wait()


def call(kernel, name, out_shape, mib, args, work, out_specs=None, scratch=(), anys=()):
    return pl.pallas_call(
        kernel,
        in_specs=[ANY if i in anys else VMEM for i in range(len(args))],
        out_specs=out_specs or [VMEM] * len(out_shape),
        out_shape=out_shape,
        scratch_shapes=list(scratch),
        compiler_params=pltpu.CompilerParams(vmem_limit_bytes=mib << 20),
        cost_estimate=pl.CostEstimate(
            flops=2 * work, bytes_accessed=work // LANES, transcendentals=0
        ),
        name=name,
    )(*args)


def ring_per_device(
    grad_out, saved_input, gate_weight, up_weight, down_weight, expert_ids, gate_num
):
    tokens_here, model_width = grad_out.shape
    local_count = lax.axis_size("local")
    experts_here, _, width = gate_weight.shape
    moves = ring_moves(local_count)
    cuts = cut_columns(2 * model_width + LANES, STREAMS)

    def shaped(*shape, dtype=jnp.bfloat16):
        return jax.ShapeDtypeStruct(shape, dtype)

    mine = lax.optimization_barrier(jnp.concatenate([saved_input, grad_out], axis=1))
    _, expert_ids = lax.optimization_barrier((mine, expert_ids))
    expert_hot = expert_ids[:, :, None] == jnp.arange(LANES, dtype=jnp.int32)[None, None, :]
    gates = jnp.sum(jnp.where(expert_hot, gate_num[:, :, None], 0), axis=1)
    gates = (gates.astype(jnp.float32) * gate_scale).astype(jnp.bfloat16)
    gathered = gather_ring(mine, gates, cuts, local_count, moves)
    half = gathered[0][0].shape[0]
    rows = 2 * half
    all_width = experts_here * width
    work = experts_here * rows * model_width * width

    def streams_of(parts):
        used = sorted({piece[0] for piece in parts})
        arrays = [value for stream in used for value in gathered[stream]]
        return arrays, [(used.index(piece[0]), *piece[1:]) for piece in parts]

    wide = shaped(rows, all_width, dtype=jnp.float32)
    in_parts = pieces(cuts, 0, model_width, model_width)
    arrays, parts = streams_of(in_parts[:1])
    sums = call(
        functools.partial(begin_kernel, parts),
        "begin",
        [wide],
        14,
        (*arrays, gate_weight),
        work,
    )
    arrays, parts = streams_of(in_parts)
    hidden, by_gate, by_up = call(
        functools.partial(finish_kernel, parts, 1),
        "finish",
        [wide] * 3,
        16,
        (*arrays, gate_weight, up_weight, *sums),
        3 * work,
    )
    arrays, parts = streams_of(
        pieces(cuts, model_width, 2 * model_width, model_width)
        + pieces(cuts, 2 * model_width, 2 * model_width + LANES, LANES)
    )
    span = cut_columns(model_width, 2)[1]
    dnear, dfar, acts, hidden = call(
        functools.partial(backward_kernel, parts[:-1], parts[-1]),
        "backward",
        [
            shaped(half, span, dtype=jnp.float32),
            shaped(half, span),
            shaped(rows, 2 * all_width),
            shaped(rows, all_width),
        ],
        24,
        (*arrays, hidden, by_gate, by_up, gate_weight, up_weight, down_weight),
        2 * work,
    )
    more_near, more_far = call(
        functools.partial(spread_kernel, span),
        "spread",
        [
            shaped(half, model_width - span, dtype=jnp.float32),
            shaped(half, model_width - span),
        ],
        16,
        (acts, gate_weight, up_weight),
        work,
    )

    def weight_grad(kernel, name, start, value, after, outs, staged):
        arrays, parts = streams_of(pieces(cuts, start, start + model_width, 1280))
        return call(
            functools.partial(kernel, parts),
            name,
            [shaped(*shape) for shape in outs],
            20,
            (*arrays, value, after),
            len(outs) * work,
            out_specs=[ANY] * len(outs),
            scratch=[
                pltpu.VMEM(staged, jnp.bfloat16),
                pltpu.SemaphoreType.DMA((len(parts), experts_here, len(outs))),
            ],
            anys=(len(arrays) + 1,),
        )

    in_shape, out_shape = (experts_here, model_width, width), (experts_here, width, model_width)
    grad_input, made = reduce_ring(
        (dnear, more_near),
        (dfar, more_far),
        local_count,
        moves,
        [
            lambda after: weight_grad(
                input_weight_kernel, "input_grads", 0, acts, after, [in_shape] * 2, (2, *in_shape)
            ),
            lambda after: weight_grad(
                down_weight_kernel, "down_grad", model_width, hidden, after, [out_shape], out_shape
            ),
        ],
    )
    made = [value for values in made for value in values]
    return (grad_input, *made)


def solution(mesh):
    per_device = ring_per_device if mesh.shape["node"] == LIMIT else slots_per_device
    in_specs = (
        P(("rep", "node", "local"), None),
        P(("rep", "node", "local"), None),
        P("node", None, "local"),
        P("node", None, "local"),
        P("node", "local", None),
        P(("rep", "node", "local"), None),
        P(("rep", "node", "local"), None),
    )
    out_specs = (
        P(("rep", "node", "local"), None),
        P(("rep", "node"), None, "local"),
        P(("rep", "node"), None, "local"),
        P(("rep", "node"), "local", None),
    )
    return jax.shard_map(
        per_device, mesh=mesh, in_specs=in_specs, out_specs=out_specs, check_vma=False
    )
```

```python
import functools

import jax
import jax.numpy as jnp
from jax import lax
from jax.experimental import pallas as pl
from jax.experimental.pallas import tpu as pltpu
from jax.sharding import PartitionSpec as P

LIMIT = 4


gate_scale = 1.0 / 256.0


def spread_rows(source, groups, local_count):
    widened = jnp.broadcast_to(source[:, None], (groups, local_count) + source.shape[1:])
    return widened.reshape((groups * local_count,) + source.shape[1:])


def slots_per_device(grad_out, saved_input, gate_weight, up_weight, down_weight, expert_ids, gate_num):
    tokens_here = grad_out.shape[0]
    model_width = grad_out.shape[1]
    groups = lax.axis_size("node")
    local_count = lax.axis_size("local")
    experts_here = gate_weight.shape[0]
    capacity = min(tokens_here, 2 * LIMIT * tokens_here // groups)
    group_of = expert_ids // experts_here
    visits = jnp.any(
        group_of[:, :, None] == jnp.arange(groups, dtype=jnp.int32)[None, None, :], axis=1
    ).astype(jnp.int32)
    before = jnp.cumsum(visits, axis=0) - visits
    slot_hit = (before[:, :, None] == jnp.arange(capacity, dtype=jnp.int32)[None, None, :]) & (
        visits[:, :, None] == 1
    )
    select = jnp.transpose(slot_hit, (1, 2, 0)).astype(jnp.bfloat16)
    expert_hot = (
        expert_ids[:, :, None] == jnp.arange(groups * experts_here, dtype=jnp.int32)[None, None, :]
    ).astype(jnp.float32)
    gate_values = jnp.sum(
        expert_hot * (gate_num.astype(jnp.float32) * gate_scale)[:, :, None], axis=1
    )
    gate_table = gate_values.reshape(tokens_here, groups, experts_here)
    send_input = jnp.einsum(
        "gct,td->gcd", select, saved_input, preferred_element_type=jnp.float32
    ).astype(jnp.bfloat16)
    send_grad = jnp.einsum(
        "gct,td->gcd", select, grad_out, preferred_element_type=jnp.float32
    ).astype(jnp.bfloat16)
    send_gate = jnp.einsum("gct,tge->gce", select.astype(jnp.float32), gate_table).astype(
        jnp.bfloat16
    )
    got_input, got_grad, got_gate = (
        lax.all_to_all(
            spread_rows(send_input, groups, local_count),
            ("node", "local"),
            split_axis=0,
            concat_axis=0,
            tiled=True,
        ),
        lax.all_to_all(
            spread_rows(send_grad, groups, local_count),
            ("node", "local"),
            split_axis=0,
            concat_axis=0,
            tiled=True,
        ),
        lax.all_to_all(
            spread_rows(send_gate, groups, local_count),
            ("node", "local"),
            split_axis=0,
            concat_axis=0,
            tiled=True,
        ),
    )
    rows_input = got_input.reshape(groups, local_count, capacity, model_width)
    rows_grad = got_grad.reshape(groups, local_count, capacity, model_width)
    rows_gate = got_gate.reshape(groups, local_count, capacity, experts_here)
    row_count = groups * local_count * capacity
    inputs = rows_input.reshape(row_count, model_width)
    row_grads = rows_grad.reshape(row_count, model_width)
    row_gates = rows_gate.reshape(row_count, experts_here)
    contract_rows = (((0,), (0,)), ((), ()))
    contract_cols = (((1,), (1,)), ((), ()))
    gate_grads = []
    up_grads = []
    down_grads = []
    pieces = []
    columns = []
    for expert in range(experts_here):
        gate_act = jnp.dot(inputs, gate_weight[expert], preferred_element_type=jnp.float32)
        up_act = jnp.dot(inputs, up_weight[expert], preferred_element_type=jnp.float32)
        sigmoid_val = jax.nn.sigmoid(gate_act)
        hidden = (gate_act * sigmoid_val * up_act).astype(jnp.bfloat16)
        scaled = (
            row_gates[:, expert : expert + 1].astype(jnp.float32) * row_grads.astype(jnp.float32)
        ).astype(jnp.bfloat16)
        down_grads.append(
            lax.dot_general(
                hidden, scaled, contract_rows, preferred_element_type=jnp.float32
            ).astype(jnp.bfloat16)
        )
        back_grad = lax.dot_general(
            scaled, down_weight[expert], contract_cols, preferred_element_type=jnp.float32
        )
        grad_gate_act = (
            back_grad * up_act * sigmoid_val * (1.0 + gate_act * (1.0 - sigmoid_val))
        ).astype(jnp.bfloat16)
        grad_up_act = (back_grad * gate_act * sigmoid_val).astype(jnp.bfloat16)
        gate_grads.append(
            lax.dot_general(
                inputs, grad_gate_act, contract_rows, preferred_element_type=jnp.float32
            ).astype(jnp.bfloat16)
        )
        up_grads.append(
            lax.dot_general(
                inputs, grad_up_act, contract_rows, preferred_element_type=jnp.float32
            ).astype(jnp.bfloat16)
        )
        pieces.append(grad_gate_act)
        pieces.append(grad_up_act)
        columns.append(gate_weight[expert])
        columns.append(up_weight[expert])
    activations = jnp.concatenate(pieces, axis=1)
    stacked = jnp.concatenate(columns, axis=1)
    partial_value = lax.dot_general(
        activations, stacked, contract_cols, preferred_element_type=jnp.float32
    )
    returned = lax.all_to_all(
        partial_value.reshape(groups * local_count, capacity, model_width),
        ("node", "local"),
        split_axis=0,
        concat_axis=0,
        tiled=True,
    )
    group_grads = jnp.sum(
        returned.reshape(groups, local_count, capacity, model_width), axis=1
    ).astype(jnp.bfloat16)
    grad_input = jnp.einsum(
        "gct,gcd->td", select, group_grads, preferred_element_type=jnp.float32
    ).astype(jnp.bfloat16)
    return (grad_input, jnp.stack(gate_grads), jnp.stack(up_grads), jnp.stack(down_grads))


LANES = 128
STREAMS = 3
NT = (((1,), (1,)), ((), ()))
TN = (((0,), (0,)), ((), ()))
VMEM = pl.BlockSpec(memory_space=pltpu.VMEM)
ANY = pl.BlockSpec(memory_space=pltpu.HBM)


def ring_moves(local_count):
    ring_len = 2 * local_count

    def place(core, spot):
        spot = spot % ring_len
        if spot < local_count:
            return core * local_count + spot
        return (2 + core) * local_count + ring_len - 1 - spot

    spots = range(ring_len)
    forth = [(place(0, i), place(0, i + 1)) for i in spots]
    forth += [(place(1, i), place(1, i - 1)) for i in spots]
    swap = [(place(core, i), place(1 - core, i)) for i in spots for core in (0, 1)]
    partner = dict(swap)
    back_swap = [(there, partner[here]) for here, there in forth]
    backs = [
        [(place(core, i), place(core, i + (2 * core - 1) * hops)) for i in spots for core in (0, 1)]
        for hops in range(local_count)
    ]
    return forth, backs, swap, back_swap


def move(value, pairs):
    return lax.ppermute(value, ("node", "local"), pairs)


def gather_ring(mine, gates, cuts, local_count, moves):
    forth, _, swap, _ = moves
    rows = mine.shape[0]
    pair = jnp.concatenate([mine, move(mine, swap)], axis=0)
    gates = jnp.concatenate([gates, move(gates, swap)], axis=0)
    blocks = [pair[:, a:b] for a, b in zip(cuts[:-1], cuts[1:], strict=True)]
    blocks[-1] = jnp.concatenate([blocks[-1], gates], axis=1)
    near = [[block[:rows]] for block in blocks]
    for _ in range(local_count - 1):
        for i, block in enumerate(blocks):
            blocks[i] = move(block, forth)
            near[i].append(blocks[i])
    for i, block in enumerate(blocks):
        near[i].append(move(block[:rows], forth))
    near = [jnp.concatenate(parts, axis=0) for parts in near]
    return [(value, move(value, swap)) for value in near]


def reduce_ring(near, far, local_count, moves, beside):
    _, backs, swap, back_swap = moves
    half = near[0].shape[0]
    rows = half // (2 * local_count)
    wide = jnp.float32
    made = []

    def with_work(moved, source):
        if len(made) < len(beside):
            moved, result = lax.optimization_barrier((moved, beside[len(made)](source)))
            made.append(result)
        return moved

    from_other = [move(value, swap) for value in far]

    def part(column, start, count):
        rows_here = slice(start, start + count)
        return near[column][rows_here].astype(wide) + from_other[column][rows_here].astype(wide)

    def own(start, count):
        return jnp.concatenate([part(i, start, count) for i in range(len(near))], axis=1)

    far_block = jnp.concatenate(
        [
            move(part(i, half - rows, rows).astype(jnp.bfloat16), backs[local_count - 1])
            for i in range(2)
        ],
        axis=1,
    )
    straight, passed = [], None
    for hops in reversed(range(1, local_count - 1)):
        at = (2 * hops + 1) * rows
        value = part(0, at, 2 * rows)
        if passed is not None:
            value = value + passed.astype(wide)
        value = value.astype(jnp.bfloat16)
        passed = move(value, backs[1])
        straight.append(move(part(1, at, 2 * rows).astype(jnp.bfloat16), backs[hops]))
    straight[-1] = with_work(straight[-1], value)
    held = [part(i, rows, 2 * rows) for i in range(2)]
    held[0] = held[0] + passed.astype(wide)
    for value in straight:
        held[1] = held[1] + value.astype(wide)
    held = jnp.concatenate(held, axis=1)
    held = jnp.concatenate([held[:rows] + far_block.astype(wide), held[rows:]], axis=0)
    held = held.astype(jnp.bfloat16)
    moving = with_work(move(held[:rows], backs[1]), held)
    crossed = move(held[rows:], back_swap)
    while len(made) < len(beside):
        made.append(beside[len(made)](held))
    total = own(0, rows) + moving.astype(wide) + crossed.astype(wide)
    return total.astype(jnp.bfloat16), made


def cut_columns(total, count):
    units = total // LANES
    return [i * units // count * LANES for i in range(count + 1)]


def pieces(cuts, start, stop, widest):
    found = []
    for stream in range(len(cuts) - 1):
        low, high = max(start, cuts[stream]), min(stop, cuts[stream + 1])
        if low >= high:
            continue
        count = -(-(high - low) // widest)
        marks = [low + at for at in cut_columns(high - low, count)]
        for a, b in zip(marks[:-1], marks[1:], strict=True):
            found.append((stream, a - cuts[stream], a - start, b - a))
    return found


def joined(refs, piece):
    stream, at, _, size = piece
    near, far = refs[2 * stream], refs[2 * stream + 1]
    return jnp.concatenate([near[:, at : at + size], far[:, at : at + size]], axis=0)


def products(parts, streams, weight_ref, expert):
    total = None
    for piece in parts:
        _, _, at, size = piece
        term = jnp.dot(
            joined(streams, piece),
            weight_ref[expert, at : at + size, :],
            preferred_element_type=jnp.float32,
        )
        total = term if total is None else total + term
    return total


def begin_kernel(parts, *refs):
    *streams, gate_ref, gate_sum_ref = refs
    experts_here, _, width = gate_ref.shape
    for expert in range(experts_here):
        cols = slice(expert * width, (expert + 1) * width)
        gate_sum_ref[:, cols] = products(parts, streams, gate_ref, expert)


def finish_kernel(parts, count, *refs):
    *streams, gate_ref, up_ref, gate_sum_ref = refs[:-3]
    hidden_ref, by_gate_ref, by_up_ref = refs[-3:]
    experts_here, _, width = up_ref.shape
    for expert in range(experts_here):
        cols = slice(expert * width, (expert + 1) * width)
        gate_act = gate_sum_ref[:, cols] + products(parts[count:], streams, gate_ref, expert)
        up_act = products(parts, streams, up_ref, expert)
        sigmoid_val = jax.nn.sigmoid(gate_act)
        silu = gate_act * sigmoid_val
        hidden_ref[:, cols] = silu * up_act
        by_gate_ref[:, cols] = up_act * sigmoid_val * (1.0 + gate_act * (1.0 - sigmoid_val))
        by_up_ref[:, cols] = silu


def backward_kernel(parts, gate_part, *refs):
    *streams, hidden_ref, by_gate_ref, by_up_ref, gate_ref, up_ref, down_ref = refs[:-4]
    dnear_ref, dfar_ref, acts_ref, hidden_out_ref = refs[-4:]
    experts_here, _, width = gate_ref.shape
    first = lax.axis_index("node") * experts_here
    gates = joined(streams, gate_part).astype(jnp.float32)
    column = lax.broadcasted_iota(jnp.int32, gates.shape, 1)
    for expert in range(experts_here):
        cols = slice(expert * width, (expert + 1) * width)
        back_grad = None
        for piece in parts:
            _, _, at, size = piece
            term = lax.dot_general(
                joined(streams, piece),
                down_ref[expert, :, at : at + size],
                NT,
                preferred_element_type=jnp.float32,
            )
            back_grad = term if back_grad is None else back_grad + term
        gate = jnp.sum(jnp.where(column == first + expert, gates, 0.0), axis=1, keepdims=True)
        back_grad = gate * back_grad
        at = 2 * expert * width
        acts_ref[:, at : at + width] = (back_grad * by_gate_ref[:, cols]).astype(jnp.bfloat16)
        acts_ref[:, at + width : at + 2 * width] = (back_grad * by_up_ref[:, cols]).astype(
            jnp.bfloat16
        )
        hidden_out_ref[:, cols] = (gate * hidden_ref[:, cols]).astype(jnp.bfloat16)
    spread(acts_ref, gate_ref, up_ref, dnear_ref, dfar_ref, 0)


def spread(acts_ref, gate_ref, up_ref, dnear_ref, dfar_ref, first):
    experts_here, _, width = gate_ref.shape
    half, span = dnear_ref.shape
    marks = cut_columns(span, -(-span // 512))
    for low, high in zip(marks[:-1], marks[1:], strict=True):
        total = None
        for expert in range(experts_here):
            for k, weight in enumerate((gate_ref, up_ref)):
                at = (2 * expert + k) * width
                term = lax.dot_general(
                    acts_ref[:, at : at + width],
                    weight[expert, first + low : first + high, :],
                    NT,
                    preferred_element_type=jnp.float32,
                )
                total = term if total is None else total + term
        dnear_ref[:, low:high] = total[:half]
        dfar_ref[:, low:high] = total[half:].astype(jnp.bfloat16)


def spread_kernel(first, acts_ref, gate_ref, up_ref, dnear_ref, dfar_ref):
    spread(acts_ref, gate_ref, up_ref, dnear_ref, dfar_ref, first)


def input_weight_kernel(parts, *refs):
    *streams, acts_ref, _, gate_out_ref, up_out_ref, staged, sem = refs
    _, experts_here, _, width = staged.shape
    copies = []
    for i, piece in enumerate(parts):
        _, _, at, size = piece
        turned = joined(streams, piece).T
        for expert in range(experts_here):
            for k, out_ref in enumerate((gate_out_ref, up_out_ref)):
                first = (2 * expert + k) * width
                staged[k, expert, at : at + size, :] = jnp.dot(
                    turned, acts_ref[:, first : first + width], preferred_element_type=jnp.float32
                ).astype(jnp.bfloat16)
                rows = pl.ds(at, size)
                copy = pltpu.make_async_copy(
                    staged.at[k, expert, rows, :], out_ref.at[expert, rows, :], sem.at[i, expert, k]
                )
                copy.start()
                copies.append(copy)
    for copy in copies:
        copy.wait()


def down_weight_kernel(parts, *refs):
    *streams, hidden_ref, _, out_ref, staged, sem = refs
    experts_here, width, _ = staged.shape
    copies = []
    turned = [
        hidden_ref[:, expert * width : (expert + 1) * width].T for expert in range(experts_here)
    ]
    for i, piece in enumerate(parts):
        _, _, at, size = piece
        grads = joined(streams, piece)
        for expert in range(experts_here):
            staged[expert, :, at : at + size] = jnp.dot(
                turned[expert], grads, preferred_element_type=jnp.float32
            ).astype(jnp.bfloat16)
            cols = pl.ds(at, size)
            copy = pltpu.make_async_copy(
                staged.at[expert, :, cols], out_ref.at[expert, :, cols], sem.at[i, expert, 0]
            )
            copy.start()
            copies.append(copy)
    for copy in copies:
        copy.wait()


def call(kernel, name, out_shape, mib, args, work, out_specs=None, scratch=(), anys=()):
    return pl.pallas_call(
        kernel,
        in_specs=[ANY if i in anys else VMEM for i in range(len(args))],
        out_specs=out_specs or [VMEM] * len(out_shape),
        out_shape=out_shape,
        scratch_shapes=list(scratch),
        compiler_params=pltpu.CompilerParams(vmem_limit_bytes=mib << 20),
        cost_estimate=pl.CostEstimate(
            flops=2 * work, bytes_accessed=work // LANES, transcendentals=0
        ),
        name=name,
    )(*args)


def ring_per_device(
    grad_out, saved_input, gate_weight, up_weight, down_weight, expert_ids, gate_num
):
    tokens_here, model_width = grad_out.shape
    local_count = lax.axis_size("local")
    experts_here, _, width = gate_weight.shape
    moves = ring_moves(local_count)
    cuts = cut_columns(2 * model_width + LANES, STREAMS)

    def shaped(*shape, dtype=jnp.bfloat16):
        return jax.ShapeDtypeStruct(shape, dtype)

    mine = lax.optimization_barrier(jnp.concatenate([saved_input, grad_out], axis=1))
    _, expert_ids = lax.optimization_barrier((mine, expert_ids))
    expert_hot = expert_ids[:, :, None] == jnp.arange(LANES, dtype=jnp.int32)[None, None, :]
    gates = jnp.sum(jnp.where(expert_hot, gate_num[:, :, None], 0), axis=1)
    gates = (gates.astype(jnp.float32) * gate_scale).astype(jnp.bfloat16)
    gathered = gather_ring(mine, gates, cuts, local_count, moves)
    half = gathered[0][0].shape[0]
    rows = 2 * half
    all_width = experts_here * width
    work = experts_here * rows * model_width * width

    def streams_of(parts):
        used = sorted({piece[0] for piece in parts})
        arrays = [value for stream in used for value in gathered[stream]]
        return arrays, [(used.index(piece[0]), *piece[1:]) for piece in parts]

    wide = shaped(rows, all_width, dtype=jnp.float32)
    in_parts = pieces(cuts, 0, model_width, model_width)
    arrays, parts = streams_of(in_parts[:1])
    sums = call(
        functools.partial(begin_kernel, parts),
        "begin",
        [wide],
        14,
        (*arrays, gate_weight),
        work,
    )
    arrays, parts = streams_of(in_parts)
    hidden, by_gate, by_up = call(
        functools.partial(finish_kernel, parts, 1),
        "finish",
        [wide] * 3,
        16,
        (*arrays, gate_weight, up_weight, *sums),
        3 * work,
    )
    arrays, parts = streams_of(
        pieces(cuts, model_width, 2 * model_width, model_width)
        + pieces(cuts, 2 * model_width, 2 * model_width + LANES, LANES)
    )
    span = cut_columns(model_width, 2)[1]
    dnear, dfar, acts, hidden = call(
        functools.partial(backward_kernel, parts[:-1], parts[-1]),
        "backward",
        [
            shaped(half, span, dtype=jnp.float32),
            shaped(half, span),
            shaped(rows, 2 * all_width),
            shaped(rows, all_width),
        ],
        24,
        (*arrays, hidden, by_gate, by_up, gate_weight, up_weight, down_weight),
        2 * work,
    )
    more_near, more_far = call(
        functools.partial(spread_kernel, span),
        "spread",
        [
            shaped(half, model_width - span, dtype=jnp.float32),
            shaped(half, model_width - span),
        ],
        16,
        (acts, gate_weight, up_weight),
        work,
    )

    def weight_grad(kernel, name, start, value, after, outs, staged):
        arrays, parts = streams_of(pieces(cuts, start, start + model_width, 1280))
        return call(
            functools.partial(kernel, parts),
            name,
            [shaped(*shape) for shape in outs],
            20,
            (*arrays, value, after),
            len(outs) * work,
            out_specs=[ANY] * len(outs),
            scratch=[
                pltpu.VMEM(staged, jnp.bfloat16),
                pltpu.SemaphoreType.DMA((len(parts), experts_here, len(outs))),
            ],
            anys=(len(arrays) + 1,),
        )

    in_shape, out_shape = (experts_here, model_width, width), (experts_here, width, model_width)
    grad_input, made = reduce_ring(
        (dnear, more_near),
        (dfar, more_far),
        local_count,
        moves,
        [
            lambda after: weight_grad(
                input_weight_kernel, "input_grads", 0, acts, after, [in_shape] * 2, (2, *in_shape)
            ),
            lambda after: weight_grad(
                down_weight_kernel, "down_grad", model_width, hidden, after, [out_shape], out_shape
            ),
        ],
    )
    made = [value for values in made for value in values]
    return (grad_input, *made)


def solution(mesh):
    every_group = mesh.shape["node"] == LIMIT and mesh.shape["local"] > 2
    per_device = ring_per_device if every_group else slots_per_device
    in_specs = (
        P(("rep", "node", "local"), None),
        P(("rep", "node", "local"), None),
        P("node", None, "local"),
        P("node", None, "local"),
        P("node", "local", None),
        P(("rep", "node", "local"), None),
        P(("rep", "node", "local"), None),
    )
    out_specs = (
        P(("rep", "node", "local"), None),
        P(("rep", "node"), None, "local"),
        P(("rep", "node"), None, "local"),
        P(("rep", "node"), "local", None),
    )
    return jax.shard_map(
        per_device, mesh=mesh, in_specs=in_specs, out_specs=out_specs, check_vma=False
    )
```

```python
import functools

import jax
import jax.numpy as jnp
from jax import lax
from jax.experimental import pallas as pl
from jax.experimental.pallas import tpu as pltpu
from jax.sharding import PartitionSpec as P

LIMIT = 4


gate_scale = 1.0 / 256.0


def spread_rows(source, groups, local_count):
    widened = jnp.broadcast_to(source[:, None], (groups, local_count) + source.shape[1:])
    return widened.reshape((groups * local_count,) + source.shape[1:])


def slots_per_device(grad_out, saved_input, gate_weight, up_weight, down_weight, expert_ids, gate_num):
    tokens_here = grad_out.shape[0]
    model_width = grad_out.shape[1]
    groups = lax.axis_size("node")
    local_count = lax.axis_size("local")
    experts_here = gate_weight.shape[0]
    capacity = min(tokens_here, 2 * LIMIT * tokens_here // groups)
    group_of = expert_ids // experts_here
    visits = jnp.any(
        group_of[:, :, None] == jnp.arange(groups, dtype=jnp.int32)[None, None, :], axis=1
    ).astype(jnp.int32)
    before = jnp.cumsum(visits, axis=0) - visits
    slot_hit = (before[:, :, None] == jnp.arange(capacity, dtype=jnp.int32)[None, None, :]) & (
        visits[:, :, None] == 1
    )
    select = jnp.transpose(slot_hit, (1, 2, 0)).astype(jnp.bfloat16)
    expert_hot = (
        expert_ids[:, :, None] == jnp.arange(groups * experts_here, dtype=jnp.int32)[None, None, :]
    ).astype(jnp.float32)
    gate_values = jnp.sum(
        expert_hot * (gate_num.astype(jnp.float32) * gate_scale)[:, :, None], axis=1
    )
    gate_table = gate_values.reshape(tokens_here, groups, experts_here)
    send_input = jnp.einsum(
        "gct,td->gcd", select, saved_input, preferred_element_type=jnp.float32
    ).astype(jnp.bfloat16)
    send_grad = jnp.einsum(
        "gct,td->gcd", select, grad_out, preferred_element_type=jnp.float32
    ).astype(jnp.bfloat16)
    send_gate = jnp.einsum("gct,tge->gce", select.astype(jnp.float32), gate_table).astype(
        jnp.bfloat16
    )
    got_input, got_grad, got_gate = (
        lax.all_to_all(
            spread_rows(send_input, groups, local_count),
            ("node", "local"),
            split_axis=0,
            concat_axis=0,
            tiled=True,
        ),
        lax.all_to_all(
            spread_rows(send_grad, groups, local_count),
            ("node", "local"),
            split_axis=0,
            concat_axis=0,
            tiled=True,
        ),
        lax.all_to_all(
            spread_rows(send_gate, groups, local_count),
            ("node", "local"),
            split_axis=0,
            concat_axis=0,
            tiled=True,
        ),
    )
    rows_input = got_input.reshape(groups, local_count, capacity, model_width)
    rows_grad = got_grad.reshape(groups, local_count, capacity, model_width)
    rows_gate = got_gate.reshape(groups, local_count, capacity, experts_here)
    row_count = groups * local_count * capacity
    inputs = rows_input.reshape(row_count, model_width)
    row_grads = rows_grad.reshape(row_count, model_width)
    row_gates = rows_gate.reshape(row_count, experts_here)
    contract_rows = (((0,), (0,)), ((), ()))
    contract_cols = (((1,), (1,)), ((), ()))
    gate_grads = []
    up_grads = []
    down_grads = []
    pieces = []
    columns = []
    for expert in range(experts_here):
        gate_act = jnp.dot(inputs, gate_weight[expert], preferred_element_type=jnp.float32)
        up_act = jnp.dot(inputs, up_weight[expert], preferred_element_type=jnp.float32)
        sigmoid_val = jax.nn.sigmoid(gate_act)
        hidden = (gate_act * sigmoid_val * up_act).astype(jnp.bfloat16)
        scaled = (
            row_gates[:, expert : expert + 1].astype(jnp.float32) * row_grads.astype(jnp.float32)
        ).astype(jnp.bfloat16)
        down_grads.append(
            lax.dot_general(
                hidden, scaled, contract_rows, preferred_element_type=jnp.float32
            ).astype(jnp.bfloat16)
        )
        back_grad = lax.dot_general(
            scaled, down_weight[expert], contract_cols, preferred_element_type=jnp.float32
        )
        grad_gate_act = (
            back_grad * up_act * sigmoid_val * (1.0 + gate_act * (1.0 - sigmoid_val))
        ).astype(jnp.bfloat16)
        grad_up_act = (back_grad * gate_act * sigmoid_val).astype(jnp.bfloat16)
        gate_grads.append(
            lax.dot_general(
                inputs, grad_gate_act, contract_rows, preferred_element_type=jnp.float32
            ).astype(jnp.bfloat16)
        )
        up_grads.append(
            lax.dot_general(
                inputs, grad_up_act, contract_rows, preferred_element_type=jnp.float32
            ).astype(jnp.bfloat16)
        )
        pieces.append(grad_gate_act)
        pieces.append(grad_up_act)
        columns.append(gate_weight[expert])
        columns.append(up_weight[expert])
    activations = jnp.concatenate(pieces, axis=1)
    stacked = jnp.concatenate(columns, axis=1)
    partial_value = lax.dot_general(
        activations, stacked, contract_cols, preferred_element_type=jnp.float32
    )
    returned = lax.all_to_all(
        partial_value.reshape(groups * local_count, capacity, model_width),
        ("node", "local"),
        split_axis=0,
        concat_axis=0,
        tiled=True,
    )
    group_grads = jnp.sum(
        returned.reshape(groups, local_count, capacity, model_width), axis=1
    ).astype(jnp.bfloat16)
    grad_input = jnp.einsum(
        "gct,gcd->td", select, group_grads, preferred_element_type=jnp.float32
    ).astype(jnp.bfloat16)
    return (grad_input, jnp.stack(gate_grads), jnp.stack(up_grads), jnp.stack(down_grads))


LANES = 128
STREAMS = 3
NT = (((1,), (1,)), ((), ()))
TN = (((0,), (0,)), ((), ()))
VMEM = pl.BlockSpec(memory_space=pltpu.VMEM)
ANY = pl.BlockSpec(memory_space=pltpu.HBM)


def ring_moves(local_count):
    ring_len = 2 * local_count

    def place(core, spot):
        spot = spot % ring_len
        if spot < local_count:
            return core * local_count + spot
        return (2 + core) * local_count + ring_len - 1 - spot

    spots = range(ring_len)
    forth = [(place(0, i), place(0, i + 1)) for i in spots]
    forth += [(place(1, i), place(1, i - 1)) for i in spots]
    swap = [(place(core, i), place(1 - core, i)) for i in spots for core in (0, 1)]
    partner = dict(swap)
    back_swap = [(there, partner[here]) for here, there in forth]
    backs = [
        [(place(core, i), place(core, i + (2 * core - 1) * hops)) for i in spots for core in (0, 1)]
        for hops in range(local_count)
    ]
    return forth, backs, swap, back_swap


def move(value, pairs):
    return lax.ppermute(value, ("node", "local"), pairs)


def gather_ring(mine, gates, cuts, local_count, moves):
    forth, _, swap, _ = moves
    rows = mine.shape[0]
    other, gates = lax.optimization_barrier((move(mine, swap), gates))
    pair = jnp.concatenate([mine, other], axis=0)
    gates = jnp.concatenate([gates, move(gates, swap)], axis=0)
    blocks = [pair[:, a:b] for a, b in zip(cuts[:-1], cuts[1:], strict=True)]
    blocks[-1] = jnp.concatenate([blocks[-1], gates], axis=1)
    near = [[block[:rows]] for block in blocks]
    for _ in range(local_count - 1):
        for i, block in enumerate(blocks):
            blocks[i] = move(block, forth)
            near[i].append(blocks[i])
    for i, block in enumerate(blocks):
        near[i].append(move(block[:rows], forth))
    near = [jnp.concatenate(parts, axis=0) for parts in near]
    return [(value, move(value, swap)) for value in near]


def reduce_ring(near, far, local_count, moves, beside):
    _, backs, swap, back_swap = moves
    half = near[0].shape[0]
    rows = half // (2 * local_count)
    wide = jnp.float32
    made = []

    def with_work(moved, source):
        if len(made) < len(beside):
            moved, result = lax.optimization_barrier((moved, beside[len(made)](source)))
            made.append(result)
        return moved

    from_other = [move(value, swap) for value in far]

    def part(column, start, count):
        rows_here = slice(start, start + count)
        return near[column][rows_here].astype(wide) + from_other[column][rows_here].astype(wide)

    def own(start, count):
        return jnp.concatenate([part(i, start, count) for i in range(len(near))], axis=1)

    last = half - rows
    far_first = move(part(0, last, rows).astype(jnp.bfloat16), backs[local_count - 2])
    far_last = move(part(1, last, rows).astype(jnp.bfloat16), backs[local_count - 1])

    def topped(value, first):
        return jnp.concatenate([value[:rows] + first.astype(wide), value[rows:]], axis=0)

    straight, passed = [], None
    for hops in reversed(range(1, local_count - 1)):
        at = (2 * hops + 1) * rows
        value = part(0, at, 2 * rows)
        if passed is not None:
            value = value + passed.astype(wide)
        if hops == 1:
            value = topped(value, far_first)
        value = value.astype(jnp.bfloat16)
        passed = move(value, backs[1])
        straight.append(move(part(1, at, 2 * rows).astype(jnp.bfloat16), backs[hops]))
    straight[0] = with_work(straight[0], value)
    held = [part(i, rows, 2 * rows) for i in range(2)]
    held[0] = held[0] + passed.astype(wide)
    for value in straight:
        held[1] = held[1] + value.astype(wide)
    held[1] = topped(held[1], far_last)
    held = jnp.concatenate(held, axis=1)
    held = held.astype(jnp.bfloat16)
    moving = move(held[:rows], backs[1])
    crossed = with_work(move(held[rows:], back_swap), held)
    while len(made) < len(beside):
        made.append(beside[len(made)](held))
    total = own(0, rows) + moving.astype(wide) + crossed.astype(wide)
    return total.astype(jnp.bfloat16), made


def cut_columns(total, count):
    units = total // LANES
    return [i * units // count * LANES for i in range(count + 1)]


def pieces(cuts, start, stop, widest):
    found = []
    for stream in range(len(cuts) - 1):
        low, high = max(start, cuts[stream]), min(stop, cuts[stream + 1])
        if low >= high:
            continue
        count = -(-(high - low) // widest)
        marks = [low + at for at in cut_columns(high - low, count)]
        for a, b in zip(marks[:-1], marks[1:], strict=True):
            found.append((stream, a - cuts[stream], a - start, b - a))
    return found


def joined(refs, piece):
    stream, at, _, size = piece
    near, far = refs[2 * stream], refs[2 * stream + 1]
    return jnp.concatenate([near[:, at : at + size], far[:, at : at + size]], axis=0)


def products(parts, streams, weight_ref, expert):
    total = None
    for piece in parts:
        _, _, at, size = piece
        term = jnp.dot(
            joined(streams, piece),
            weight_ref[expert, at : at + size, :],
            preferred_element_type=jnp.float32,
        )
        total = term if total is None else total + term
    return total


def begin_kernel(parts, *refs):
    *streams, gate_ref, gate_sum_ref = refs
    experts_here, _, width = gate_ref.shape
    for expert in range(experts_here):
        cols = slice(expert * width, (expert + 1) * width)
        gate_sum_ref[:, cols] = products(parts, streams, gate_ref, expert)


def finish_kernel(parts, count, *refs):
    *streams, gate_ref, up_ref, gate_sum_ref = refs[:-3]
    hidden_ref, by_gate_ref, by_up_ref = refs[-3:]
    experts_here, _, width = up_ref.shape
    for expert in range(experts_here):
        cols = slice(expert * width, (expert + 1) * width)
        gate_act = gate_sum_ref[:, cols] + products(parts[count:], streams, gate_ref, expert)
        up_act = products(parts, streams, up_ref, expert)
        sigmoid_val = jax.nn.sigmoid(gate_act)
        silu = gate_act * sigmoid_val
        hidden_ref[:, cols] = silu * up_act
        by_gate_ref[:, cols] = up_act * sigmoid_val * (1.0 + gate_act * (1.0 - sigmoid_val))
        by_up_ref[:, cols] = silu


def backward_kernel(parts, gate_part, *refs):
    *streams, hidden_ref, by_gate_ref, by_up_ref, gate_ref, up_ref, down_ref = refs[:-4]
    dnear_ref, dfar_ref, acts_ref, hidden_out_ref = refs[-4:]
    experts_here, _, width = gate_ref.shape
    first = lax.axis_index("node") * experts_here
    gates = joined(streams, gate_part).astype(jnp.float32)
    column = lax.broadcasted_iota(jnp.int32, gates.shape, 1)
    for expert in range(experts_here):
        cols = slice(expert * width, (expert + 1) * width)
        back_grad = None
        for piece in parts:
            _, _, at, size = piece
            term = lax.dot_general(
                joined(streams, piece),
                down_ref[expert, :, at : at + size],
                NT,
                preferred_element_type=jnp.float32,
            )
            back_grad = term if back_grad is None else back_grad + term
        gate = jnp.sum(jnp.where(column == first + expert, gates, 0.0), axis=1, keepdims=True)
        back_grad = gate * back_grad
        at = 2 * expert * width
        acts_ref[:, at : at + width] = (back_grad * by_gate_ref[:, cols]).astype(jnp.bfloat16)
        acts_ref[:, at + width : at + 2 * width] = (back_grad * by_up_ref[:, cols]).astype(
            jnp.bfloat16
        )
        hidden_out_ref[:, cols] = (gate * hidden_ref[:, cols]).astype(jnp.bfloat16)
    spread(acts_ref, gate_ref, up_ref, dnear_ref, dfar_ref, 0)


def spread(acts_ref, gate_ref, up_ref, dnear_ref, dfar_ref, first):
    experts_here, _, width = gate_ref.shape
    half, span = dnear_ref.shape
    marks = cut_columns(span, -(-span // 512))
    for low, high in zip(marks[:-1], marks[1:], strict=True):
        total = None
        for expert in range(experts_here):
            for k, weight in enumerate((gate_ref, up_ref)):
                at = (2 * expert + k) * width
                term = lax.dot_general(
                    acts_ref[:, at : at + width],
                    weight[expert, first + low : first + high, :],
                    NT,
                    preferred_element_type=jnp.float32,
                )
                total = term if total is None else total + term
        dnear_ref[:, low:high] = total[:half]
        dfar_ref[:, low:high] = total[half:].astype(jnp.bfloat16)


def spread_kernel(first, acts_ref, gate_ref, up_ref, dnear_ref, dfar_ref):
    spread(acts_ref, gate_ref, up_ref, dnear_ref, dfar_ref, first)


def input_weight_kernel(parts, *refs):
    *streams, acts_ref, _, gate_out_ref, up_out_ref, staged, sem = refs
    _, experts_here, _, width = staged.shape
    copies = []
    for i, piece in enumerate(parts):
        _, _, at, size = piece
        turned = joined(streams, piece).T
        for expert in range(experts_here):
            for k, out_ref in enumerate((gate_out_ref, up_out_ref)):
                first = (2 * expert + k) * width
                staged[k, expert, at : at + size, :] = jnp.dot(
                    turned, acts_ref[:, first : first + width], preferred_element_type=jnp.float32
                ).astype(jnp.bfloat16)
                rows = pl.ds(at, size)
                copy = pltpu.make_async_copy(
                    staged.at[k, expert, rows, :], out_ref.at[expert, rows, :], sem.at[i, expert, k]
                )
                copy.start()
                copies.append(copy)
    for copy in copies:
        copy.wait()


def down_weight_kernel(parts, *refs):
    *streams, hidden_ref, _, out_ref, staged, sem = refs
    experts_here, width, _ = staged.shape
    copies = []
    turned = [
        hidden_ref[:, expert * width : (expert + 1) * width].T for expert in range(experts_here)
    ]
    for i, piece in enumerate(parts):
        _, _, at, size = piece
        grads = joined(streams, piece)
        for expert in range(experts_here):
            staged[expert, :, at : at + size] = jnp.dot(
                turned[expert], grads, preferred_element_type=jnp.float32
            ).astype(jnp.bfloat16)
            cols = pl.ds(at, size)
            copy = pltpu.make_async_copy(
                staged.at[expert, :, cols], out_ref.at[expert, :, cols], sem.at[i, expert, 0]
            )
            copy.start()
            copies.append(copy)
    for copy in copies:
        copy.wait()


def call(kernel, name, out_shape, mib, args, work, out_specs=None, scratch=(), anys=()):
    return pl.pallas_call(
        kernel,
        in_specs=[ANY if i in anys else VMEM for i in range(len(args))],
        out_specs=out_specs or [VMEM] * len(out_shape),
        out_shape=out_shape,
        scratch_shapes=list(scratch),
        compiler_params=pltpu.CompilerParams(vmem_limit_bytes=mib << 20),
        cost_estimate=pl.CostEstimate(
            flops=2 * work, bytes_accessed=work // LANES, transcendentals=0
        ),
        name=name,
    )(*args)


def ring_per_device(
    grad_out, saved_input, gate_weight, up_weight, down_weight, expert_ids, gate_num
):
    tokens_here, model_width = grad_out.shape
    local_count = lax.axis_size("local")
    experts_here, _, width = gate_weight.shape
    moves = ring_moves(local_count)
    cuts = cut_columns(2 * model_width + LANES, STREAMS)

    def shaped(*shape, dtype=jnp.bfloat16):
        return jax.ShapeDtypeStruct(shape, dtype)

    mine = lax.optimization_barrier(jnp.concatenate([saved_input, grad_out], axis=1))
    _, expert_ids = lax.optimization_barrier((mine, expert_ids))
    expert_hot = expert_ids[:, :, None] == jnp.arange(LANES, dtype=jnp.int32)[None, None, :]
    gates = jnp.sum(jnp.where(expert_hot, gate_num[:, :, None], 0), axis=1)
    gates = (gates.astype(jnp.float32) * gate_scale).astype(jnp.bfloat16)
    gathered = gather_ring(mine, gates, cuts, local_count, moves)
    half = gathered[0][0].shape[0]
    rows = 2 * half
    all_width = experts_here * width
    work = experts_here * rows * model_width * width

    def streams_of(parts):
        used = sorted({piece[0] for piece in parts})
        arrays = [value for stream in used for value in gathered[stream]]
        return arrays, [(used.index(piece[0]), *piece[1:]) for piece in parts]

    wide = shaped(rows, all_width, dtype=jnp.float32)
    in_parts = pieces(cuts, 0, model_width, model_width)
    arrays, parts = streams_of(in_parts[:1])
    sums = call(
        functools.partial(begin_kernel, parts),
        "begin",
        [wide],
        14,
        (*arrays, gate_weight),
        work,
    )
    arrays, parts = streams_of(in_parts)
    hidden, by_gate, by_up = call(
        functools.partial(finish_kernel, parts, 1),
        "finish",
        [wide] * 3,
        16,
        (*arrays, gate_weight, up_weight, *sums),
        3 * work,
    )
    arrays, parts = streams_of(
        pieces(cuts, model_width, 2 * model_width, model_width)
        + pieces(cuts, 2 * model_width, 2 * model_width + LANES, LANES)
    )
    span = cut_columns(model_width, 2)[1]
    dnear, dfar, acts, hidden = call(
        functools.partial(backward_kernel, parts[:-1], parts[-1]),
        "backward",
        [
            shaped(half, span, dtype=jnp.float32),
            shaped(half, span),
            shaped(rows, 2 * all_width),
            shaped(rows, all_width),
        ],
        24,
        (*arrays, hidden, by_gate, by_up, gate_weight, up_weight, down_weight),
        2 * work,
    )
    more_near, more_far = call(
        functools.partial(spread_kernel, span),
        "spread",
        [
            shaped(half, model_width - span, dtype=jnp.float32),
            shaped(half, model_width - span),
        ],
        16,
        (acts, gate_weight, up_weight),
        work,
    )

    def weight_grad(kernel, name, start, value, after, outs, staged):
        arrays, parts = streams_of(pieces(cuts, start, start + model_width, 1280))
        return call(
            functools.partial(kernel, parts),
            name,
            [shaped(*shape) for shape in outs],
            20,
            (*arrays, value, after),
            len(outs) * work,
            out_specs=[ANY] * len(outs),
            scratch=[
                pltpu.VMEM(staged, jnp.bfloat16),
                pltpu.SemaphoreType.DMA((len(parts), experts_here, len(outs))),
            ],
            anys=(len(arrays) + 1,),
        )

    in_shape, out_shape = (experts_here, model_width, width), (experts_here, width, model_width)
    grad_input, made = reduce_ring(
        (dnear, more_near),
        (dfar, more_far),
        local_count,
        moves,
        [
            lambda after: weight_grad(
                input_weight_kernel, "input_grads", 0, acts, after, [in_shape] * 2, (2, *in_shape)
            ),
            lambda after: weight_grad(
                down_weight_kernel, "down_grad", model_width, hidden, after, [out_shape], out_shape
            ),
        ],
    )
    made = [value for values in made for value in values]
    return (grad_input, *made)


def solution(mesh):
    every_group = mesh.shape["node"] == LIMIT and mesh.shape["local"] > 2
    per_device = ring_per_device if every_group else slots_per_device
    in_specs = (
        P(("rep", "node", "local"), None),
        P(("rep", "node", "local"), None),
        P("node", None, "local"),
        P("node", None, "local"),
        P("node", "local", None),
        P(("rep", "node", "local"), None),
        P(("rep", "node", "local"), None),
    )
    out_specs = (
        P(("rep", "node", "local"), None),
        P(("rep", "node"), None, "local"),
        P(("rep", "node"), None, "local"),
        P(("rep", "node"), "local", None),
    )
    return jax.shard_map(
        per_device, mesh=mesh, in_specs=in_specs, out_specs=out_specs, check_vma=False
    )
```

```python
import functools

import jax
import jax.numpy as jnp
from jax import lax
from jax.experimental import pallas as pl
from jax.experimental.pallas import tpu as pltpu
from jax.sharding import PartitionSpec as P

LIMIT = 4


gate_scale = 1.0 / 256.0


def spread_rows(source, groups, local_count):
    widened = jnp.broadcast_to(source[:, None], (groups, local_count) + source.shape[1:])
    return widened.reshape((groups * local_count,) + source.shape[1:])


def slots_per_device(grad_out, saved_input, gate_weight, up_weight, down_weight, expert_ids, gate_num):
    tokens_here = grad_out.shape[0]
    model_width = grad_out.shape[1]
    groups = lax.axis_size("node")
    local_count = lax.axis_size("local")
    experts_here = gate_weight.shape[0]
    capacity = min(tokens_here, 2 * LIMIT * tokens_here // groups)
    group_of = expert_ids // experts_here
    visits = jnp.any(
        group_of[:, :, None] == jnp.arange(groups, dtype=jnp.int32)[None, None, :], axis=1
    ).astype(jnp.int32)
    before = jnp.cumsum(visits, axis=0) - visits
    slot_hit = (before[:, :, None] == jnp.arange(capacity, dtype=jnp.int32)[None, None, :]) & (
        visits[:, :, None] == 1
    )
    select = jnp.transpose(slot_hit, (1, 2, 0)).astype(jnp.bfloat16)
    expert_hot = (
        expert_ids[:, :, None] == jnp.arange(groups * experts_here, dtype=jnp.int32)[None, None, :]
    ).astype(jnp.float32)
    gate_values = jnp.sum(
        expert_hot * (gate_num.astype(jnp.float32) * gate_scale)[:, :, None], axis=1
    )
    gate_table = gate_values.reshape(tokens_here, groups, experts_here)
    send_input = jnp.einsum(
        "gct,td->gcd", select, saved_input, preferred_element_type=jnp.float32
    ).astype(jnp.bfloat16)
    send_grad = jnp.einsum(
        "gct,td->gcd", select, grad_out, preferred_element_type=jnp.float32
    ).astype(jnp.bfloat16)
    send_gate = jnp.einsum("gct,tge->gce", select.astype(jnp.float32), gate_table).astype(
        jnp.bfloat16
    )
    got_input, got_grad, got_gate = (
        lax.all_to_all(
            spread_rows(send_input, groups, local_count),
            ("node", "local"),
            split_axis=0,
            concat_axis=0,
            tiled=True,
        ),
        lax.all_to_all(
            spread_rows(send_grad, groups, local_count),
            ("node", "local"),
            split_axis=0,
            concat_axis=0,
            tiled=True,
        ),
        lax.all_to_all(
            spread_rows(send_gate, groups, local_count),
            ("node", "local"),
            split_axis=0,
            concat_axis=0,
            tiled=True,
        ),
    )
    rows_input = got_input.reshape(groups, local_count, capacity, model_width)
    rows_grad = got_grad.reshape(groups, local_count, capacity, model_width)
    rows_gate = got_gate.reshape(groups, local_count, capacity, experts_here)
    row_count = groups * local_count * capacity
    inputs = rows_input.reshape(row_count, model_width)
    row_grads = rows_grad.reshape(row_count, model_width)
    row_gates = rows_gate.reshape(row_count, experts_here)
    contract_rows = (((0,), (0,)), ((), ()))
    contract_cols = (((1,), (1,)), ((), ()))
    gate_grads = []
    up_grads = []
    down_grads = []
    pieces = []
    columns = []
    for expert in range(experts_here):
        gate_act = jnp.dot(inputs, gate_weight[expert], preferred_element_type=jnp.float32)
        up_act = jnp.dot(inputs, up_weight[expert], preferred_element_type=jnp.float32)
        sigmoid_val = jax.nn.sigmoid(gate_act)
        hidden = (gate_act * sigmoid_val * up_act).astype(jnp.bfloat16)
        scaled = (
            row_gates[:, expert : expert + 1].astype(jnp.float32) * row_grads.astype(jnp.float32)
        ).astype(jnp.bfloat16)
        down_grads.append(
            lax.dot_general(
                hidden, scaled, contract_rows, preferred_element_type=jnp.float32
            ).astype(jnp.bfloat16)
        )
        back_grad = lax.dot_general(
            scaled, down_weight[expert], contract_cols, preferred_element_type=jnp.float32
        )
        grad_gate_act = (
            back_grad * up_act * sigmoid_val * (1.0 + gate_act * (1.0 - sigmoid_val))
        ).astype(jnp.bfloat16)
        grad_up_act = (back_grad * gate_act * sigmoid_val).astype(jnp.bfloat16)
        gate_grads.append(
            lax.dot_general(
                inputs, grad_gate_act, contract_rows, preferred_element_type=jnp.float32
            ).astype(jnp.bfloat16)
        )
        up_grads.append(
            lax.dot_general(
                inputs, grad_up_act, contract_rows, preferred_element_type=jnp.float32
            ).astype(jnp.bfloat16)
        )
        pieces.append(grad_gate_act)
        pieces.append(grad_up_act)
        columns.append(gate_weight[expert])
        columns.append(up_weight[expert])
    activations = jnp.concatenate(pieces, axis=1)
    stacked = jnp.concatenate(columns, axis=1)
    partial_value = lax.dot_general(
        activations, stacked, contract_cols, preferred_element_type=jnp.float32
    )
    returned = lax.all_to_all(
        partial_value.reshape(groups * local_count, capacity, model_width),
        ("node", "local"),
        split_axis=0,
        concat_axis=0,
        tiled=True,
    )
    group_grads = jnp.sum(
        returned.reshape(groups, local_count, capacity, model_width), axis=1
    ).astype(jnp.bfloat16)
    grad_input = jnp.einsum(
        "gct,gcd->td", select, group_grads, preferred_element_type=jnp.float32
    ).astype(jnp.bfloat16)
    return (grad_input, jnp.stack(gate_grads), jnp.stack(up_grads), jnp.stack(down_grads))


LANES = 128
STREAMS = 3
NT = (((1,), (1,)), ((), ()))
TN = (((0,), (0,)), ((), ()))
VMEM = pl.BlockSpec(memory_space=pltpu.VMEM)
ANY = pl.BlockSpec(memory_space=pltpu.HBM)


def ring_moves(local_count):
    ring_len = 2 * local_count

    def place(core, spot):
        spot = spot % ring_len
        if spot < local_count:
            return core * local_count + spot
        return (2 + core) * local_count + ring_len - 1 - spot

    spots = range(ring_len)
    forth = [(place(0, i), place(0, i + 1)) for i in spots]
    forth += [(place(1, i), place(1, i - 1)) for i in spots]
    swap = [(place(core, i), place(1 - core, i)) for i in spots for core in (0, 1)]
    partner = dict(swap)
    back_swap = [(there, partner[here]) for here, there in forth]
    backs = [
        [(place(core, i), place(core, i + (2 * core - 1) * hops)) for i in spots for core in (0, 1)]
        for hops in range(local_count)
    ]
    return forth, backs, swap, back_swap


def move(value, pairs):
    return lax.ppermute(value, ("node", "local"), pairs)


def gather_ring(mine, gates, cuts, local_count, moves):
    forth, _, swap, _ = moves
    rows = mine.shape[0]
    other, gates = lax.optimization_barrier((move(mine, swap), gates))
    pair = jnp.concatenate([mine, other], axis=0)
    gates = jnp.concatenate([gates, move(gates, swap)], axis=0)
    blocks = [pair[:, a:b] for a, b in zip(cuts[:-1], cuts[1:], strict=True)]
    blocks[-1] = jnp.concatenate([blocks[-1], gates], axis=1)
    near = [[block[:rows]] for block in blocks]
    for _ in range(local_count - 1):
        for i, block in enumerate(blocks):
            blocks[i] = move(block, forth)
            near[i].append(blocks[i])
    for i, block in enumerate(blocks):
        near[i].append(move(block[:rows], forth))
    near = [jnp.concatenate(parts, axis=0) for parts in near]
    return [(value, move(value, swap)) for value in near]


def reduce_ring(near, far, local_count, moves, beside):
    _, backs, swap, back_swap = moves
    half = near[0].shape[0]
    rows = half // (2 * local_count)
    wide = jnp.float32
    made = []

    def with_work(moved, source):
        if len(made) < len(beside):
            moved, result = lax.optimization_barrier((moved, beside[len(made)](source)))
            made.append(result)
        return moved

    from_other = [move(value, swap) for value in far]

    def part(column, start, count):
        rows_here = slice(start, start + count)
        return near[column][rows_here].astype(wide) + from_other[column][rows_here].astype(wide)

    def own(start, count):
        return jnp.concatenate([part(i, start, count) for i in range(len(near))], axis=1)

    last = half - rows
    far_first = move(part(0, last, rows).astype(jnp.bfloat16), backs[local_count - 2])
    far_last = move(part(1, last, rows).astype(jnp.bfloat16), backs[local_count - 1])

    def topped(value, first):
        return jnp.concatenate([value[:rows] + first.astype(wide), value[rows:]], axis=0)

    straight, passed = [], None
    for hops in reversed(range(1, local_count - 1)):
        at = (2 * hops + 1) * rows
        value = part(0, at, 2 * rows)
        if passed is not None:
            value = value + passed.astype(wide)
        if hops == 1:
            value = topped(value, far_first)
        value = value.astype(jnp.bfloat16)
        passed = move(value, backs[1])
        straight.append(move(part(1, at, 2 * rows).astype(jnp.bfloat16), backs[hops]))
    straight[-1], passed = with_work((straight[-1], passed), value)
    held = [part(i, rows, 2 * rows) for i in range(2)]
    held[0] = held[0] + passed.astype(wide)
    for value in straight:
        held[1] = held[1] + value.astype(wide)
    held[1] = topped(held[1], far_last)
    held = jnp.concatenate(held, axis=1)
    held = held.astype(jnp.bfloat16)
    moving = move(held[:rows], backs[1])
    crossed = with_work(move(held[rows:], back_swap), held)
    while len(made) < len(beside):
        made.append(beside[len(made)](held))
    total = own(0, rows) + moving.astype(wide) + crossed.astype(wide)
    return total.astype(jnp.bfloat16), made


def cut_columns(total, count):
    units = total // LANES
    return [i * units // count * LANES for i in range(count + 1)]


def pieces(cuts, start, stop, widest):
    found = []
    for stream in range(len(cuts) - 1):
        low, high = max(start, cuts[stream]), min(stop, cuts[stream + 1])
        if low >= high:
            continue
        count = -(-(high - low) // widest)
        marks = [low + at for at in cut_columns(high - low, count)]
        for a, b in zip(marks[:-1], marks[1:], strict=True):
            found.append((stream, a - cuts[stream], a - start, b - a))
    return found


def joined(refs, piece):
    stream, at, _, size = piece
    near, far = refs[2 * stream], refs[2 * stream + 1]
    return jnp.concatenate([near[:, at : at + size], far[:, at : at + size]], axis=0)


def products(parts, streams, weight_ref, expert):
    total = None
    for piece in parts:
        _, _, at, size = piece
        term = jnp.dot(
            joined(streams, piece),
            weight_ref[expert, at : at + size, :],
            preferred_element_type=jnp.float32,
        )
        total = term if total is None else total + term
    return total


def begin_kernel(parts, *refs):
    *streams, gate_ref, gate_sum_ref = refs
    experts_here, _, width = gate_ref.shape
    for expert in range(experts_here):
        cols = slice(expert * width, (expert + 1) * width)
        gate_sum_ref[:, cols] = products(parts, streams, gate_ref, expert)


def finish_kernel(parts, count, *refs):
    *streams, gate_ref, up_ref, gate_sum_ref = refs[:-3]
    hidden_ref, by_gate_ref, by_up_ref = refs[-3:]
    experts_here, _, width = up_ref.shape
    for expert in range(experts_here):
        cols = slice(expert * width, (expert + 1) * width)
        gate_act = gate_sum_ref[:, cols] + products(parts[count:], streams, gate_ref, expert)
        up_act = products(parts, streams, up_ref, expert)
        sigmoid_val = jax.nn.sigmoid(gate_act)
        silu = gate_act * sigmoid_val
        hidden_ref[:, cols] = silu * up_act
        by_gate_ref[:, cols] = up_act * sigmoid_val * (1.0 + gate_act * (1.0 - sigmoid_val))
        by_up_ref[:, cols] = silu


def backward_kernel(parts, gate_part, *refs):
    *streams, hidden_ref, by_gate_ref, by_up_ref, gate_ref, up_ref, down_ref = refs[:-4]
    dnear_ref, dfar_ref, acts_ref, hidden_out_ref = refs[-4:]
    experts_here, _, width = gate_ref.shape
    first = lax.axis_index("node") * experts_here
    gates = joined(streams, gate_part).astype(jnp.float32)
    column = lax.broadcasted_iota(jnp.int32, gates.shape, 1)
    for expert in range(experts_here):
        cols = slice(expert * width, (expert + 1) * width)
        back_grad = None
        for piece in parts:
            _, _, at, size = piece
            term = lax.dot_general(
                joined(streams, piece),
                down_ref[expert, :, at : at + size],
                NT,
                preferred_element_type=jnp.float32,
            )
            back_grad = term if back_grad is None else back_grad + term
        gate = jnp.sum(jnp.where(column == first + expert, gates, 0.0), axis=1, keepdims=True)
        back_grad = gate * back_grad
        at = 2 * expert * width
        acts_ref[:, at : at + width] = (back_grad * by_gate_ref[:, cols]).astype(jnp.bfloat16)
        acts_ref[:, at + width : at + 2 * width] = (back_grad * by_up_ref[:, cols]).astype(
            jnp.bfloat16
        )
        hidden_out_ref[:, cols] = (gate * hidden_ref[:, cols]).astype(jnp.bfloat16)
    spread(acts_ref, gate_ref, up_ref, dnear_ref, dfar_ref, 0)


def spread(acts_ref, gate_ref, up_ref, dnear_ref, dfar_ref, first):
    experts_here, _, width = gate_ref.shape
    half, span = dnear_ref.shape
    marks = cut_columns(span, -(-span // 512))
    for low, high in zip(marks[:-1], marks[1:], strict=True):
        total = None
        for expert in range(experts_here):
            for k, weight in enumerate((gate_ref, up_ref)):
                at = (2 * expert + k) * width
                term = lax.dot_general(
                    acts_ref[:, at : at + width],
                    weight[expert, first + low : first + high, :],
                    NT,
                    preferred_element_type=jnp.float32,
                )
                total = term if total is None else total + term
        dnear_ref[:, low:high] = total[:half]
        dfar_ref[:, low:high] = total[half:].astype(jnp.bfloat16)


def spread_kernel(first, acts_ref, gate_ref, up_ref, dnear_ref, dfar_ref):
    spread(acts_ref, gate_ref, up_ref, dnear_ref, dfar_ref, first)


def input_weight_kernel(parts, *refs):
    *streams, acts_ref, _, gate_out_ref, up_out_ref, staged, sem = refs
    _, experts_here, _, width = staged.shape
    copies = []
    for i, piece in enumerate(parts):
        _, _, at, size = piece
        turned = joined(streams, piece).T
        for expert in range(experts_here):
            for k, out_ref in enumerate((gate_out_ref, up_out_ref)):
                first = (2 * expert + k) * width
                staged[k, expert, at : at + size, :] = jnp.dot(
                    turned, acts_ref[:, first : first + width], preferred_element_type=jnp.float32
                ).astype(jnp.bfloat16)
                rows = pl.ds(at, size)
                copy = pltpu.make_async_copy(
                    staged.at[k, expert, rows, :], out_ref.at[expert, rows, :], sem.at[i, expert, k]
                )
                copy.start()
                copies.append(copy)
    for copy in copies:
        copy.wait()


def down_weight_kernel(parts, *refs):
    *streams, hidden_ref, _, out_ref, staged, sem = refs
    experts_here, width, _ = staged.shape
    copies = []
    turned = [
        hidden_ref[:, expert * width : (expert + 1) * width].T for expert in range(experts_here)
    ]
    for i, piece in enumerate(parts):
        _, _, at, size = piece
        grads = joined(streams, piece)
        for expert in range(experts_here):
            staged[expert, :, at : at + size] = jnp.dot(
                turned[expert], grads, preferred_element_type=jnp.float32
            ).astype(jnp.bfloat16)
            cols = pl.ds(at, size)
            copy = pltpu.make_async_copy(
                staged.at[expert, :, cols], out_ref.at[expert, :, cols], sem.at[i, expert, 0]
            )
            copy.start()
            copies.append(copy)
    for copy in copies:
        copy.wait()


def call(kernel, name, out_shape, mib, args, work, out_specs=None, scratch=(), anys=()):
    return pl.pallas_call(
        kernel,
        in_specs=[ANY if i in anys else VMEM for i in range(len(args))],
        out_specs=out_specs or [VMEM] * len(out_shape),
        out_shape=out_shape,
        scratch_shapes=list(scratch),
        compiler_params=pltpu.CompilerParams(vmem_limit_bytes=mib << 20),
        cost_estimate=pl.CostEstimate(
            flops=2 * work, bytes_accessed=work // LANES, transcendentals=0
        ),
        name=name,
    )(*args)


def ring_per_device(
    grad_out, saved_input, gate_weight, up_weight, down_weight, expert_ids, gate_num
):
    tokens_here, model_width = grad_out.shape
    local_count = lax.axis_size("local")
    experts_here, _, width = gate_weight.shape
    moves = ring_moves(local_count)
    cuts = cut_columns(2 * model_width + LANES, STREAMS)

    def shaped(*shape, dtype=jnp.bfloat16):
        return jax.ShapeDtypeStruct(shape, dtype)

    mine = lax.optimization_barrier(jnp.concatenate([saved_input, grad_out], axis=1))
    _, expert_ids = lax.optimization_barrier((mine, expert_ids))
    expert_hot = expert_ids[:, :, None] == jnp.arange(LANES, dtype=jnp.int32)[None, None, :]
    gates = jnp.sum(jnp.where(expert_hot, gate_num[:, :, None], 0), axis=1)
    gates = (gates.astype(jnp.float32) * gate_scale).astype(jnp.bfloat16)
    gathered = gather_ring(mine, gates, cuts, local_count, moves)
    half = gathered[0][0].shape[0]
    rows = 2 * half
    all_width = experts_here * width
    work = experts_here * rows * model_width * width

    def streams_of(parts):
        used = sorted({piece[0] for piece in parts})
        arrays = [value for stream in used for value in gathered[stream]]
        return arrays, [(used.index(piece[0]), *piece[1:]) for piece in parts]

    wide = shaped(rows, all_width, dtype=jnp.float32)
    in_parts = pieces(cuts, 0, model_width, model_width)
    arrays, parts = streams_of(in_parts[:1])
    sums = call(
        functools.partial(begin_kernel, parts),
        "begin",
        [wide],
        14,
        (*arrays, gate_weight),
        work,
    )
    arrays, parts = streams_of(in_parts)
    hidden, by_gate, by_up = call(
        functools.partial(finish_kernel, parts, 1),
        "finish",
        [wide] * 3,
        16,
        (*arrays, gate_weight, up_weight, *sums),
        3 * work,
    )
    arrays, parts = streams_of(
        pieces(cuts, model_width, 2 * model_width, model_width)
        + pieces(cuts, 2 * model_width, 2 * model_width + LANES, LANES)
    )
    span = cut_columns(model_width, 2)[1]
    dnear, dfar, acts, hidden = call(
        functools.partial(backward_kernel, parts[:-1], parts[-1]),
        "backward",
        [
            shaped(half, span, dtype=jnp.float32),
            shaped(half, span),
            shaped(rows, 2 * all_width),
            shaped(rows, all_width),
        ],
        24,
        (*arrays, hidden, by_gate, by_up, gate_weight, up_weight, down_weight),
        2 * work,
    )
    more_near, more_far = call(
        functools.partial(spread_kernel, span),
        "spread",
        [
            shaped(half, model_width - span, dtype=jnp.float32),
            shaped(half, model_width - span),
        ],
        16,
        (acts, gate_weight, up_weight),
        work,
    )

    def weight_grad(kernel, name, start, value, after, outs, staged):
        arrays, parts = streams_of(pieces(cuts, start, start + model_width, 1280))
        return call(
            functools.partial(kernel, parts),
            name,
            [shaped(*shape) for shape in outs],
            20,
            (*arrays, value, after),
            len(outs) * work,
            out_specs=[ANY] * len(outs),
            scratch=[
                pltpu.VMEM(staged, jnp.bfloat16),
                pltpu.SemaphoreType.DMA((len(parts), experts_here, len(outs))),
            ],
            anys=(len(arrays) + 1,),
        )

    in_shape, out_shape = (experts_here, model_width, width), (experts_here, width, model_width)
    grad_input, made = reduce_ring(
        (dnear, more_near),
        (dfar, more_far),
        local_count,
        moves,
        [
            lambda after: weight_grad(
                input_weight_kernel, "input_grads", 0, acts, after, [in_shape] * 2, (2, *in_shape)
            ),
            lambda after: weight_grad(
                down_weight_kernel, "down_grad", model_width, hidden, after, [out_shape], out_shape
            ),
        ],
    )
    made = [value for values in made for value in values]
    return (grad_input, *made)


def solution(mesh):
    every_group = mesh.shape["node"] == LIMIT and mesh.shape["local"] > 2
    per_device = ring_per_device if every_group else slots_per_device
    in_specs = (
        P(("rep", "node", "local"), None),
        P(("rep", "node", "local"), None),
        P("node", None, "local"),
        P("node", None, "local"),
        P("node", "local", None),
        P(("rep", "node", "local"), None),
        P(("rep", "node", "local"), None),
    )
    out_specs = (
        P(("rep", "node", "local"), None),
        P(("rep", "node"), None, "local"),
        P(("rep", "node"), None, "local"),
        P(("rep", "node"), "local", None),
    )
    return jax.shard_map(
        per_device, mesh=mesh, in_specs=in_specs, out_specs=out_specs, check_vma=False
    )
```
